128 devices in a mesh: leaf: 8 (over x, core), space: 16 (over y, z).
Axes of the slice: x: 4, y: 4, z: 4, core: 2. Of those that a mesh axis runs over, the one named last changes fastest.
Arguments:
- basis: bfloat16 [8, 262144, 256], P('leaf', 'space'), may hold values from -6 to 6
- sing_vals: float32 [8, 256], P('leaf'), may hold values from 0.7 to 1.4
- sketch: float32 [512, 256], replicated, may hold values from -6 to 6
Outputs:
- fresh: bfloat16 [8, 262144, 256], P('leaf', 'space')
- correlation: float32 [8, 256, 256], P('leaf')
The draws below stay inside these ranges and needn't reach their ends.
All inputs are finite; a program needn't handle non-finite values.
Results may differ from the reference program's by a relative error of at most 0.012.
Values may be sent and summed in bfloat16 or wider, within the bound.
A program may use at most 128 MiB of HBM per device.

```python
import math
import jax
import jax.numpy as jnp
from jax import lax

K = 256
MERGED = 512
ITERS = 2
POINTS = 262144
GROUPS = 8


def draw_basis(key, part):
    key = jax.random.fold_in(key, 11)
    key_common, key_own, key_share = jax.random.split(key, 3)
    common = jnp.clip(jax.random.normal(key_common, (1, POINTS, K), jnp.float32), -4.0, 4.0)
    own = jnp.clip(jax.random.normal(key_own, (GROUPS, POINTS, K), jnp.float32), -4.0, 4.0)
    share = jax.random.uniform(key_share, (GROUPS, 1, K), jnp.float32, 0.5, 0.7)
    mixed = share * common + jnp.sqrt(1.0 - share * share) * own
    return jnp.clip(mixed, -6.0, 6.0).astype(jnp.bfloat16)


def levels(stream_key, extent, pieces, smallest, high):
    factor_of, own = 1.0, jax.random.fold_in(stream_key, 6)
    for axis_at, parts in pieces:
        steps = jnp.exp(jax.random.uniform(jax.random.fold_in(own, axis_at), (parts,), jnp.float32, smallest / len(pieces), high / len(pieces)))
        factor_of = factor_of * jnp.repeat(steps, extent[axis_at] // parts).reshape([-1 if axis == axis_at else 1 for axis in range(len(extent))])
    return factor_of


def centred(own_key, extent, width, limit, held_as=jnp.bfloat16):
    result = jax.random.normal(own_key, extent, jnp.float32) * width
    return jnp.minimum(jnp.maximum(result, -limit), limit).astype(held_as)


def setup_inputs(seed: int = 0) -> dict:
    key_of = jax.random.split(jax.random.key(seed), 4)
    return {
        "basis": draw_basis(jax.random.fold_in(key_of[3], 71), 0),
        "sing_vals": jnp.clip(jnp.exp(math.log(1.4) - 0.6931472 * jax.random.uniform(key_of[1], (GROUPS, K), jnp.float32) ** levels(key_of[1], (GROUPS, K), ((0, 8),), -0.2, 0.2)), 0.7, 1.4),
        "sketch": centred(key_of[2], (MERGED, K), 1.0, 6.0, jnp.float32),
    }


def orthonormal(block):
    inner = jnp.dot(block.T, block, precision=lax.Precision.HIGHEST)
    lower = jnp.linalg.cholesky(inner)
    return lax.linalg.triangular_solve(lower, block, left_side=False, lower=True, transpose_a=True)

def reference(basis, sing_vals, sketch):
    scaled = (basis.astype(jnp.float32) * sing_vals[:, None, :]).astype(jnp.bfloat16)
    contract = (((0,), (0,)), ((), ()))

    def merge_pair(index):
        even = scaled[2 * index]
        odd = scaled[2 * index + 1]
        merged = jnp.concatenate([even, odd], axis=1)
        gram = lax.dot_general(merged.astype(jnp.float32), merged.astype(jnp.float32), contract, preferred_element_type=jnp.float32)
        block = sketch
        for step in range(ITERS):
            block = orthonormal(jnp.dot(gram, block, precision=lax.Precision.HIGHEST))
        block_b = block.astype(jnp.bfloat16)
        fresh_pair = jnp.dot(merged.astype(jnp.float32), block_b.astype(jnp.float32), preferred_element_type=jnp.float32).astype(jnp.bfloat16)
        weights = block_b.astype(jnp.float32)
        cross_even = lax.dot_general(even.astype(jnp.float32), merged.astype(jnp.float32), contract, preferred_element_type=jnp.float32)
        cross_odd = lax.dot_general(odd.astype(jnp.float32), merged.astype(jnp.float32), contract, preferred_element_type=jnp.float32)
        over_even = jnp.dot(cross_even, weights, precision=lax.Precision.HIGHEST) / POINTS
        over_odd = jnp.dot(cross_odd, weights, precision=lax.Precision.HIGHEST) / POINTS
        return (fresh_pair, jnp.stack([over_even, over_odd]))
    fresh_pairs, correlations = lax.map(merge_pair, jnp.arange(GROUPS // 2, dtype=jnp.int32))
    fresh = jnp.repeat(fresh_pairs, 2, axis=0)
    correlation = correlations.reshape(GROUPS, K, K)
    return (fresh, correlation)
```

```python
import jax
import jax.numpy as jnp
from jax import lax
from jax.sharding import PartitionSpec as P

ITERS = 2


def from_partner(value, axis, stride):
    return lax.ppermute(value, axis, [(i, i ^ 1 << stride) for i in range(lax.axis_size(axis))])


def orthonormal(block):
    inner = jnp.dot(block.T, block, precision=lax.Precision.HIGHEST)
    lower = jnp.linalg.cholesky(inner)
    return lax.linalg.triangular_solve(lower, block, left_side=False, lower=True, transpose_a=True)


def on_device(basis, sing_vals, sketch):
    contract = (((0,), (0,)), ((), ()))
    points = basis.shape[1] * lax.axis_size("space")
    own = (basis[0].astype(jnp.float32) * sing_vals[0][None, :]).astype(jnp.bfloat16)
    other = from_partner(own, "leaf", 0)
    is_even = lax.axis_index("leaf") % 2 == 0
    even = jnp.where(is_even, own, other)
    odd = jnp.where(is_even, other, own)
    merged = jnp.concatenate([even, odd], axis=1)
    local_gram = lax.dot_general(merged, merged, contract, preferred_element_type=jnp.float32)
    gram = lax.psum(local_gram, "space")
    block = sketch
    for step in range(ITERS):
        block = orthonormal(jnp.dot(gram, block, precision=lax.Precision.HIGHEST))
    block_b = block.astype(jnp.bfloat16)
    weights = block_b.astype(jnp.float32)
    fresh = jnp.dot(merged, block_b, preferred_element_type=jnp.float32).astype(jnp.bfloat16)
    own_rows = lax.dynamic_slice_in_dim(gram, (lax.axis_index("leaf") % 2) * own.shape[1], own.shape[1], 0)
    correlation = jnp.dot(own_rows, weights, precision=lax.Precision.HIGHEST) / points
    return (fresh[None], correlation[None])


def solution(mesh):
    in_specs = (P("leaf", "space", None), P("leaf", None), P())
    out_specs = (P("leaf", "space", None), P("leaf", None, None))
    return jax.shard_map(
        on_device, mesh=mesh, in_specs=in_specs, out_specs=out_specs, check_vma=False
    )
```

```python
import functools
import jax
import jax.numpy as jnp
from jax import lax
from jax.experimental import pallas as pl
from jax.experimental.pallas import tpu as pltpu
from jax.sharding import PartitionSpec as P

ITERS = 2
PANEL = 32
SUB = 16
EXACT = lax.Precision.HIGHEST


def dot(a, b, on_a, on_b, precision=EXACT):
    dims = (((on_a,), (on_b,)), ((), ()))
    return lax.dot_general(a, b, dims, precision=precision, preferred_element_type=jnp.float32)


def inverse_factor(inner):
    n = inner.shape[0]
    count = n // PANEL
    wide = n // 128
    lane = lax.broadcasted_iota(jnp.int32, (PANEL, n), 1)
    row = lax.broadcasted_iota(jnp.int32, (PANEL, 128), 0)
    row_wide = lax.broadcasted_iota(jnp.int32, (PANEL, n), 0)
    panels = [inner[i * PANEL : (i + 1) * PANEL] for i in range(count)]
    done = []
    for p in range(count):
        w = panels[p]
        first = p * PANEL
        diag = jnp.zeros((PANEL, 128), jnp.float32)
        for sub in range(0, PANEL, SUB):
            cols = [
                jnp.broadcast_to(w[:, first + sub + j : first + sub + j + 1], (PANEL, 128))
                for j in range(SUB)
            ]
            for j in range(SUB):
                at = sub + j
                top = at // 8 * 8
                inv = (1.0 / jnp.broadcast_to(cols[j][at : at + 1], (8, 128)))[0:1]
                mult = jnp.where(row[top:] > at, cols[j][top:] * inv, 0.0)
                for k in range(j + 1, SUB):
                    low = cols[k][top:] - mult * cols[k][at : at + 1]
                    cols[k] = jnp.concatenate([cols[k][:top], low], axis=0) if top else low
                diag = jnp.where(row == at, cols[j], diag)
                unit = jnp.where(row_wide[top:] == at, 1.0, 0.0)
                low = jnp.where(lane[top:] == first + at, unit, w[top:])
                low = low - jnp.concatenate([mult] * wide, axis=1) * low[at - top : at - top + 1]
                if top:
                    low = jnp.concatenate(
                        [jnp.where(lane[:top] == first + at, 0.0, w[:top]), low], axis=0
                    )
                w = low
        w = w * jnp.concatenate([lax.rsqrt(diag)] * wide, axis=1)
        done.append(jnp.where(lane < first + PANEL, w, 0.0) if p + 1 < count else w)
        blank = (lane >= first) & (lane < first + PANEL)
        if p + 1 < count:
            after = first + PANEL
            near = dot(w[:, after : after + PANEL], w, 0, 0)
            panels[p + 1] = jnp.where(blank, 0.0, panels[p + 1]) - near
        if p + 2 < count:
            far = dot(w[:, after + PANEL :], w, 0, 0)
            for m in range(p + 2, count):
                at = (m - p - 2) * PANEL
                panels[m] = jnp.where(blank, 0.0, panels[m]) - far[at : at + PANEL]
    return jnp.concatenate(done, axis=0)


def subspace_kernel(points, gram_ref, sketch_ref, own_ref, q_ref, corr_ref):
    gram = gram_ref[...]
    block = sketch_ref[...].T
    for _ in range(ITERS):
        y = dot(block, gram, 1, 0)
        block = dot(inverse_factor(dot(y, y, 1, 1)), y, 1, 0)
    q_b = block.T.astype(jnp.bfloat16)
    q_ref[...] = q_b
    corr_ref[...] = dot(own_ref[...], q_b.astype(jnp.float32), 1, 0) * (1.0 / points)


def from_partner(value, axis, stride):
    return lax.ppermute(value, axis, [(i, i ^ 1 << stride) for i in range(lax.axis_size(axis))])


def on_device(basis, sing_vals, sketch):
    contract = (((0,), (0,)), ((), ()))
    points = basis.shape[1] * lax.axis_size("space")
    own = (basis[0].astype(jnp.float32) * sing_vals[0][None, :]).astype(jnp.bfloat16)
    other = from_partner(own, "leaf", 0)
    is_even = lax.axis_index("leaf") % 2 == 0
    even = jnp.where(is_even, own, other)
    odd = jnp.where(is_even, other, own)
    merged = jnp.concatenate([even, odd], axis=1)
    local_gram = lax.dot_general(merged, merged, contract, preferred_element_type=jnp.float32)
    gram = lax.psum(local_gram, "space")
    kept = own.shape[1]
    own_rows = lax.dynamic_slice_in_dim(gram, (lax.axis_index("leaf") % 2) * kept, kept, 0)
    block_b, correlation = pl.pallas_call(
        functools.partial(subspace_kernel, points),
        out_shape=(
            jax.ShapeDtypeStruct(sketch.shape, jnp.bfloat16),
            jax.ShapeDtypeStruct((kept, kept), jnp.float32),
        ),
        compiler_params=pltpu.CompilerParams(vmem_limit_bytes=32 * 1024 * 1024),
        name="subspace",
    )(gram, sketch, own_rows)
    fresh = jnp.dot(merged, block_b, preferred_element_type=jnp.float32).astype(jnp.bfloat16)
    return (fresh[None], correlation[None])


def solution(mesh):
    in_specs = (P("leaf", "space", None), P("leaf", None), P())
    out_specs = (P("leaf", "space", None), P("leaf", None, None))
    return jax.shard_map(
        on_device, mesh=mesh, in_specs=in_specs, out_specs=out_specs, check_vma=False
    )
```

```python
import functools
import jax
import jax.numpy as jnp
from jax import lax
from jax.experimental import pallas as pl
from jax.experimental.pallas import tpu as pltpu
from jax.sharding import PartitionSpec as P

ITERS = 2
PANEL = 32
SUB = 16
CHUNK = 2048
TILE = 2048
MESH = pl.DeviceIdType.MESH
EXACT = lax.Precision.HIGHEST


def dot(a, b, on_a, on_b, precision=EXACT):
    dims = (((on_a,), (on_b,)), ((), ()))
    return lax.dot_general(a, b, dims, precision=precision, preferred_element_type=jnp.float32)


def inverse_factor(inner):
    n = inner.shape[0]
    count = n // PANEL
    wide = n // 128
    lane = lax.broadcasted_iota(jnp.int32, (PANEL, n), 1)
    row = lax.broadcasted_iota(jnp.int32, (PANEL, 128), 0)
    row_wide = lax.broadcasted_iota(jnp.int32, (PANEL, n), 0)
    panels = [inner[i * PANEL : (i + 1) * PANEL] for i in range(count)]
    done = []
    for p in range(count):
        w = panels[p]
        first = p * PANEL
        diag = jnp.zeros((PANEL, 128), jnp.float32)
        for sub in range(0, PANEL, SUB):
            cols = [
                jnp.broadcast_to(w[:, first + sub + j : first + sub + j + 1], (PANEL, 128))
                for j in range(SUB)
            ]
            for j in range(SUB):
                at = sub + j
                top = at // 8 * 8
                inv = (1.0 / jnp.broadcast_to(cols[j][at : at + 1], (8, 128)))[0:1]
                mult = jnp.where(row[top:] > at, cols[j][top:] * inv, 0.0)
                for k in range(j + 1, SUB):
                    low = cols[k][top:] - mult * cols[k][at : at + 1]
                    cols[k] = jnp.concatenate([cols[k][:top], low], axis=0) if top else low
                diag = jnp.where(row == at, cols[j], diag)
                unit = jnp.where(row_wide[top:] == at, 1.0, 0.0)
                low = jnp.where(lane[top:] == first + at, unit, w[top:])
                low = low - jnp.concatenate([mult] * wide, axis=1) * low[at - top : at - top + 1]
                if top:
                    low = jnp.concatenate(
                        [jnp.where(lane[:top] == first + at, 0.0, w[:top]), low], axis=0
                    )
                w = low
        w = w * jnp.concatenate([lax.rsqrt(diag)] * wide, axis=1)
        done.append(jnp.where(lane < first + PANEL, w, 0.0) if p + 1 < count else w)
        blank = (lane >= first) & (lane < first + PANEL)
        if p + 1 < count:
            after = first + PANEL
            near = dot(w[:, after : after + PANEL], w, 0, 0)
            panels[p + 1] = jnp.where(blank, 0.0, panels[p + 1]) - near
        if p + 2 < count:
            far = dot(w[:, after + PANEL :], w, 0, 0)
            for m in range(p + 2, count):
                at = (m - p - 2) * PANEL
                panels[m] = jnp.where(blank, 0.0, panels[m]) - far[at : at + PANEL]
    return jnp.concatenate(done, axis=0)


def exchange_kernel(
    basis_ref, sing_ref, own_a, own_b, other_a, diag_ref, cross_ref,
    turned, acc, acc_x, out_own, in_own, out_x, in_x,
    load_sem, swap_send, swap_recv, send_sems, recv_sems,
):
    leaf, space = lax.axis_index("leaf"), lax.axis_index("space")
    spaces = lax.axis_size("space")
    peers = 2 * spaces
    core, pair = lax.rem(leaf, 2), lax.div(leaf, 2)
    me = space * 2 + core
    partner = (leaf + 1 - 2 * core, space)
    half = own_a.shape[0]
    chunks = half // CHUNK

    def peer(d):
        to = lax.rem(me + d, peers)
        return lax.rem(to, 2), lax.div(to, 2)

    def load(part, start, i):
        rows = pl.ds(pl.multiple_of(i * CHUNK, CHUNK), CHUNK)
        source = pl.ds(pl.multiple_of(start + i * CHUNK, CHUNK), CHUNK)
        return part.at[rows], basis_ref.at[0, source]

    first, second = (1 - core) * half, core * half
    for i in range(chunks):
        to, source = load(own_a, first, i)
        pltpu.make_async_copy(source, to, load_sem.at[i]).start()
    for i in range(chunks):
        to, source = load(own_b, second, i)
        pltpu.make_async_copy(source, to, load_sem.at[chunks + i]).start()

    barrier = pltpu.get_barrier_semaphore()

    @pl.loop(1, peers)
    def _(d):
        to_core, to_space = peer(d)
        pl.semaphore_signal(
            barrier, inc=1, device_id=(pair * 2 + to_core, to_space), device_id_type=MESH
        )

    acc[...] = jnp.zeros_like(acc)
    acc_x[...] = jnp.zeros_like(acc_x)
    scale = sing_ref[...]

    def scaled(part, i, start, sem):
        to, source = load(part, start, i)
        pltpu.make_async_copy(source, to, sem).wait()
        rows = pl.ds(pl.multiple_of(i * CHUNK, CHUNK), CHUNK)
        part[rows, :] = (part[rows, :].astype(jnp.float32) * scale).astype(jnp.bfloat16)
        return rows

    def swap(i):
        rows = pl.ds(pl.multiple_of(i * CHUNK, CHUNK), CHUNK)
        return pltpu.make_async_remote_copy(
            src_ref=own_a.at[rows], dst_ref=other_a.at[rows], send_sem=swap_send.at[i],
            recv_sem=swap_recv.at[i], device_id=partner, device_id_type=MESH,
        )

    def send(src, dst, which, to_core, to_space):
        pltpu.make_async_remote_copy(
            src_ref=src, dst_ref=dst, send_sem=send_sems.at[which], recv_sem=recv_sems.at[which],
            device_id=(pair * 2 + to_core, to_space), device_id_type=MESH,
        ).start()

    def landed(ref, sem):
        pltpu.make_async_copy(ref, ref, sem).wait()

    scaled(own_a, 0, first, load_sem.at[0])
    pl.semaphore_wait(barrier, peers - 1)
    swap(0).start()

    @pl.loop(1, chunks)
    def _(i):
        scaled(own_a, i, first, load_sem.at[i])
        swap(i).start()

    @pl.loop(0, chunks)
    def _(i):
        rows = pl.ds(pl.multiple_of(i * CHUNK, CHUNK), CHUNK)
        value = own_a[rows, :]
        acc[...] += dot(value, value, 0, 0, None)

    @pl.loop(0, chunks)
    def _(i):
        rows = scaled(own_b, i, second, load_sem.at[chunks + i])
        value = own_b[rows, :]
        flipped = value.T
        turned[i] = flipped
        acc[...] += dot(flipped, value, 1, 0, None)

    out_own[...] = acc[...].astype(out_own.dtype).reshape(out_own.shape)

    @pl.loop(1, spaces)
    def _(d):
        to = lax.rem(space + d, spaces)
        send(out_own.at[to], in_own.at[d - 1], 0, core, to)

    @pl.loop(0, chunks)
    def _(i):
        swap(i).wait_recv()
        rows = pl.ds(pl.multiple_of(i * CHUNK, CHUNK), CHUNK)
        acc_x[...] += dot(turned[i], other_a[rows, :], 1, 0, None)

    cross = acc_x[...]
    cross = jnp.where(core == 0, cross, cross.T).astype(out_x.dtype)
    wide = cross.shape[1] // 2
    out_x[0] = cross[:, :wide].reshape(out_x.shape[1:])
    out_x[1] = cross[:, wide:].reshape(out_x.shape[1:])

    @pl.loop(1, peers)
    def _(d):
        to_core, to_space = peer(d)
        send(out_x.at[to_core, to_space], in_x.at[d - 1], 1, to_core, to_space)

    landed(in_own, recv_sems.at[0])
    mine = acc[pl.ds(pl.multiple_of(space * 16, 16), 16), :]
    diag_ref[me] = mine + jnp.sum(in_own[...].astype(jnp.float32), axis=0)

    @pl.loop(1, peers)
    def _(d):
        to_core, to_space = peer(d)
        send(diag_ref.at[me], diag_ref.at[me], 2, to_core, to_space)

    landed(in_x, recv_sems.at[1])
    mine = out_x[core, space].astype(jnp.float32)
    cross_ref[me] = mine + jnp.sum(in_x[...].astype(jnp.float32), axis=0)

    @pl.loop(1, peers)
    def _(d):
        to_core, to_space = peer(d)
        send(cross_ref.at[me], cross_ref.at[me], 3, to_core, to_space)

    landed(diag_ref.at[pl.ds(0, peers - 1)], recv_sems.at[2])
    landed(cross_ref.at[pl.ds(0, peers - 1)], recv_sems.at[3])
    landed(in_own, send_sems.at[0])
    landed(in_x, send_sems.at[1])
    landed(diag_ref.at[pl.ds(0, peers - 1)], send_sems.at[2])
    landed(cross_ref.at[pl.ds(0, peers - 1)], send_sems.at[3])

    @pl.loop(0, chunks)
    def _(i):
        swap(i).wait_send()


def subspace_kernel(points, diag_ref, cross_ref, sketch_ref, q_ref, corr_ref, gram):
    k = corr_ref.shape[0]
    diag = diag_ref[...].reshape(k // 16, 2, 16, k)
    cross = cross_ref[...].reshape(k // 16, 2, 16, k // 2)
    corner = jnp.concatenate([cross[:, c].reshape(k, k // 2) for c in range(2)], axis=1)
    gram[:k, :k] = diag[:, 0].reshape(k, k)
    gram[k:, k:] = diag[:, 1].reshape(k, k)
    gram[:k, k:] = corner
    gram[k:, :k] = corner.T
    block = sketch_ref[...].T
    for _ in range(ITERS):
        y = dot(block, gram[...], 1, 0)
        block = dot(inverse_factor(dot(y, y, 1, 1)), y, 1, 0)
    q_b = block.T.astype(jnp.bfloat16)
    q_ref[...] = q_b
    own = pl.multiple_of(lax.rem(lax.axis_index("leaf"), 2) * k, k)
    corr_ref[...] = dot(gram[pl.ds(own, k), :], q_b.astype(jnp.float32), 1, 0) * (1.0 / points)


def fresh_kernel(own_a, own_b, other_a, other_b, q_ref, fresh_ref, held, sem):
    core = lax.rem(lax.axis_index("leaf"), 2)
    half, k = own_a.shape
    own = pl.ds(pl.multiple_of(core * k, k), k)
    rest = pl.ds(pl.multiple_of((1 - core) * k, k), k)
    weights = jnp.concatenate([q_ref[own, :], q_ref[rest, :]], axis=0)
    copies = []
    for part, (mine, other) in enumerate(((own_a, other_b), (own_b, other_a))):
        start = (1 - core if part == 0 else core) * half
        for i in range(half // TILE):
            rows = pl.ds(i * TILE, TILE)
            at = pl.ds(part * half + i * TILE, TILE)
            merged = jnp.concatenate([mine[rows, :], other[rows, :]], axis=1)
            held[at, :] = dot(merged, weights, 1, 0, None).astype(jnp.bfloat16)
            to = fresh_ref.at[0, pl.ds(pl.multiple_of(start + i * TILE, TILE), TILE)]
            copies.append(pltpu.make_async_copy(held.at[at], to, sem.at[len(copies)]))
            copies[-1].start()
    for copy in copies:
        copy.wait()


def from_partner(value, axis, stride):
    return lax.ppermute(value, axis, [(i, i ^ 1 << stride) for i in range(lax.axis_size(axis))])


def on_device(basis, sing_vals, sketch):
    rows, k = basis.shape[1:]
    spaces = lax.axis_size("space")
    points = rows * spaces
    half = rows // 2
    vmem = pl.BlockSpec(memory_space=pltpu.VMEM)
    any_space = pl.BlockSpec(memory_space=pl.ANY)
    f32, wire = jnp.float32, jnp.bfloat16
    chunks = half // CHUNK
    own_a, own_b, other_a, diag, cross = pl.pallas_call(
        exchange_kernel,
        out_shape=(
            pltpu.VMEM((half, k), jnp.bfloat16),
            pltpu.VMEM((half, k), jnp.bfloat16),
            pltpu.VMEM((half, k), jnp.bfloat16),
            pltpu.VMEM((2 * spaces, k // spaces, k), f32),
            pltpu.VMEM((2 * spaces, k // spaces, k // 2), f32),
        ),
        in_specs=[pl.BlockSpec(memory_space=pltpu.HBM), vmem],
        out_specs=(vmem,) * 5,
        scratch_shapes=[
            pltpu.VMEM((chunks, k, CHUNK), jnp.bfloat16),
            pltpu.VMEM((k, k), f32),
            pltpu.VMEM((k, k), f32),
            pltpu.VMEM((spaces, k // spaces, k), wire),
            pltpu.VMEM((spaces - 1, k // spaces, k), wire),
            pltpu.VMEM((2, spaces, k // spaces, k // 2), wire),
            pltpu.VMEM((2 * spaces - 1, k // spaces, k // 2), wire),
            pltpu.SemaphoreType.DMA((2 * chunks,)),
            pltpu.SemaphoreType.DMA((chunks,)),
            pltpu.SemaphoreType.DMA((chunks,)),
            pltpu.SemaphoreType.DMA((4,)),
            pltpu.SemaphoreType.DMA((4,)),
        ],
        compiler_params=pltpu.CompilerParams(
            collective_id=0, has_side_effects=True, vmem_limit_bytes=36 * 2**20
        ),
        name="exchange",
    )(basis, sing_vals)
    other_b = from_partner(own_b, "leaf", 0)
    block_b, correlation = pl.pallas_call(
        functools.partial(subspace_kernel, points),
        out_shape=(
            jax.ShapeDtypeStruct(sketch.shape, jnp.bfloat16),
            jax.ShapeDtypeStruct((k, k), f32),
        ),
        in_specs=[vmem, vmem, vmem],
        out_specs=(vmem, vmem),
        scratch_shapes=[pltpu.VMEM((2 * k, 2 * k), f32)],
        compiler_params=pltpu.CompilerParams(vmem_limit_bytes=16 * 2**20),
        cost_estimate=pl.CostEstimate(flops=2**31, bytes_accessed=80 * 2**20, transcendentals=0),
        name="subspace",
    )(diag, cross, sketch)
    fresh = pl.pallas_call(
        fresh_kernel,
        out_shape=jax.ShapeDtypeStruct((1, rows, k), jnp.bfloat16),
        in_specs=[vmem] * 5,
        out_specs=any_space,
        scratch_shapes=[
            pltpu.VMEM((rows, k), jnp.bfloat16),
            pltpu.SemaphoreType.DMA((rows // TILE,)),
        ],
        compiler_params=pltpu.CompilerParams(vmem_limit_bytes=32 * 2**20),
        name="fresh",
    )(own_a, own_b, other_a, other_b, block_b)
    return (fresh, correlation[None])


def solution(mesh):
    in_specs = (P("leaf", "space", None), P("leaf", None), P())
    out_specs = (P("leaf", "space", None), P("leaf", None, None))
    return jax.shard_map(
        on_device, mesh=mesh, in_specs=in_specs, out_specs=out_specs, check_vma=False
    )
```

```python
import functools
import jax
import jax.numpy as jnp
from jax import lax
from jax.experimental import pallas as pl
from jax.experimental.pallas import tpu as pltpu
from jax.sharding import PartitionSpec as P

ITERS = 2
PANEL = 32
SUB = 16
CHUNK = 1024
STRIP = 2048
TILE = 2048
MESH = pl.DeviceIdType.MESH
EXACT = lax.Precision.HIGH


def dot(a, b, on_a, on_b, precision=EXACT):
    dims = (((on_a,), (on_b,)), ((), ()))
    return lax.dot_general(a, b, dims, precision=precision, preferred_element_type=jnp.float32)


def stack(block):
    terms = []
    for _ in range(3):
        terms.append(block.astype(jnp.bfloat16))
        block = block - terms[-1].astype(jnp.float32)
    high, mid, low = terms
    left = jnp.concatenate([high, mid, high, mid, low, high], axis=0)
    return left, jnp.concatenate([high, high, mid, mid, high, low], axis=0)


def inverse_factor(inner):
    n = inner.shape[0]
    count = n // PANEL
    tile = (8, 128)
    tall, wide = PANEL // 8, n // 128
    lane = lax.broadcasted_iota(jnp.int32, tile, 1)
    row = lax.broadcasted_iota(jnp.int32, tile, 0)
    lane_wide = lax.broadcasted_iota(jnp.int32, (PANEL, n), 1)
    unit = [jnp.where(row == s, 1.0, 0.0) for s in range(8)]
    panels = [inner[i * PANEL : (i + 1) * PANEL] for i in range(count)]
    done = []
    for p in range(count):
        first = p * PANEL
        here, base = first // 128, first % 128
        w = [
            [panels[p][8 * r : 8 * r + 8, 128 * h : 128 * h + 128] for h in range(wide)]
            for r in range(tall)
        ]
        diag = [jnp.zeros(tile, jnp.float32)] * tall
        for sub in range(0, PANEL, SUB):
            cols = [
                {
                    r: jnp.broadcast_to(w[r][here][:, base + sub + j : base + sub + j + 1], tile)
                    for r in range(sub // 8, tall)
                }
                for j in range(SUB)
            ]
            for j in range(SUB):
                at = sub + j
                top, s = at // 8, at % 8
                inv = 1.0 / jnp.broadcast_to(cols[j][top][s : s + 1], tile)
                mult = {r: cols[j][r] * inv for r in range(top, tall)}
                mult[top] = jnp.where(row > s, mult[top], 0.0)
                if s == 7:
                    del mult[top]
                for k in range(j + 1, SUB):
                    pivot = cols[k][top][s : s + 1]
                    for r in mult:
                        cols[k][r] = cols[k][r] - mult[r] * pivot
                diag[top] = jnp.where(row == s, cols[j][top], diag[top])
                at_lane = lane == base + at
                w[top][here] = jnp.where(at_lane, unit[s], w[top][here])
                for r in range(top + 1, tall):
                    w[r][here] = jnp.where(at_lane, 0.0, w[r][here])
                for h in range(wide):
                    pivot = w[top][h][s : s + 1]
                    for r in mult:
                        w[r][h] = w[r][h] - mult[r] * pivot
        for r in range(tall):
            scale = lax.rsqrt(diag[r])
            w[r] = [value * scale for value in w[r]]
            if r + 1 < tall:
                above = (lane >= base + 8 * r + 8) & (lane < base + PANEL)
                w[r][here] = jnp.where(above, 0.0, w[r][here])
        block = jnp.concatenate([jnp.concatenate(tiles, axis=1) for tiles in w], axis=0)
        after = first + PANEL
        if after == n:
            done.append(block)
            break
        done.append(jnp.where(lane_wide < after, block, 0.0))
        blank = (lane_wide >= first) & (lane_wide < after)
        left, right = stack(block)
        near = dot(left[:, after : after + PANEL], right, 0, 0, None)
        panels[p + 1] = jnp.where(blank, 0.0, panels[p + 1]) - near
        if after + PANEL < n:
            far = dot(left[:, after + PANEL :], right, 0, 0, None)
            for m in range(p + 2, count):
                at = (m - p - 2) * PANEL
                panels[m] = jnp.where(blank, 0.0, panels[m]) - far[at : at + PANEL]
    return jnp.concatenate(done, axis=0)


def exchange_kernel(
    basis_ref, sing_ref, own_a, own_b, other_a, diag_ref, cross_ref,
    sing, turned, acc, acc_x, out_own, in_own, out_x, in_x,
    answer, entered, sing_sem, load_sem, swap_send, swap_recv, send_sems, recv_sems,
):
    leaf, space = lax.axis_index("leaf"), lax.axis_index("space")
    spaces = lax.axis_size("space")
    peers = 2 * spaces
    core, pair = lax.rem(leaf, 2), lax.div(leaf, 2)
    me = space * 2 + core
    partner = (leaf + 1 - 2 * core, space)
    half = own_a.shape[0]
    chunks, strips = half // CHUNK, half // STRIP

    def away(i):
        side = 4
        k, m = lax.div(i, side), lax.rem(i, side)
        dy = lax.rem(2 + k + lax.div(k, 2) * (5 - 2 * k), side)
        dz = lax.rem(2 + m + lax.div(m, 2) * (5 - 2 * m), side)
        y, z = lax.div(space, side), lax.rem(space, side)
        return lax.rem(y + dy, side) * side + lax.rem(z + dz, side)

    def span(i, size, start=0):
        return pl.ds(pl.multiple_of(start + i * size, size), size)

    def load(part, start, i, size, sem):
        return pltpu.make_async_copy(
            basis_ref.at[0, span(i, size, start)], part.at[span(i, size)], sem
        )

    def scale(part, i, size):
        rows = span(i, size)
        part[rows, :] = (part[rows, :].astype(jnp.float32) * sing[...]).astype(jnp.bfloat16)

    def swap(i):
        return pltpu.make_async_remote_copy(
            src_ref=own_a.at[span(i, CHUNK)], dst_ref=other_a.at[span(i, CHUNK)],
            send_sem=swap_send.at[i], recv_sem=swap_recv.at[i],
            device_id=partner, device_id_type=MESH,
        )

    def send(src, dst, which, to_core, to_space):
        pltpu.make_async_remote_copy(
            src_ref=src, dst_ref=dst, send_sem=send_sems.at[which], recv_sem=recv_sems.at[which],
            device_id=(pair * 2 + to_core, to_space), device_id_type=MESH,
        ).start()

    def landed(ref, sem):
        pltpu.make_async_copy(ref, ref, sem).wait()

    sing_copy = pltpu.make_async_copy(sing_ref, sing, sing_sem)
    sing_copy.start()
    first, second = (1 - core) * half, core * half
    for i in range(chunks):
        load(own_a, first, i, CHUNK, load_sem.at[i]).start()
    for i in range(strips):
        load(own_b, second, i, STRIP, load_sem.at[chunks + i]).start()

    barrier = pltpu.get_barrier_semaphore()

    @pl.when(core == 1)
    def _():
        pl.semaphore_signal(barrier, inc=1, device_id=partner, device_id_type=MESH)

    @pl.when(core == 0)
    def _():
        pl.semaphore_wait(barrier, 1)
        pl.semaphore_signal(answer, inc=1, device_id=partner, device_id_type=MESH)

    @pl.when(core == 1)
    def _():
        pl.semaphore_wait(answer, 1)

        @pl.loop(0, spaces - 1)
        def _(i):
            pl.semaphore_signal(
                barrier, inc=1, device_id=(leaf, away(i)), device_id_type=MESH
            )

    acc[...] = jnp.zeros_like(acc)
    acc_x[...] = jnp.zeros_like(acc_x)
    sing_copy.wait()
    load(own_a, first, 0, CHUNK, load_sem.at[0]).wait()
    scale(own_a, 0, CHUNK)
    swap(0).start()

    @pl.loop(1, chunks)
    def _(i):
        load(own_a, first, i, CHUNK, load_sem.at[i]).wait()
        scale(own_a, i, CHUNK)
        swap(i).start()

    @pl.loop(0, strips)
    def _(i):
        value = own_a[span(i, STRIP), :]
        acc[...] += dot(value, value, 0, 0, None)

    @pl.loop(0, strips)
    def _(i):
        load(own_b, second, i, STRIP, load_sem.at[chunks + i]).wait()
        scale(own_b, i, STRIP)
        value = own_b[span(i, STRIP), :]
        flipped = value.T
        for part in range(STRIP // CHUNK):
            turned[i * (STRIP // CHUNK) + part] = flipped[:, part * CHUNK : (part + 1) * CHUNK]
        acc[...] += dot(flipped, value, 1, 0, None)

    @pl.when(core == 1)
    def _():
        pl.semaphore_wait(barrier, spaces - 1)
        pl.semaphore_signal(entered, inc=1, device_id=partner, device_id_type=MESH)

    @pl.when(core == 0)
    def _():
        pl.semaphore_wait(entered, 1)

    out_own[...] = acc[...].astype(out_own.dtype).reshape(out_own.shape)

    @pl.loop(0, spaces - 1)
    def _(i):
        to = away(i)
        send(out_own.at[to], in_own.at[i], 0, core, to)

    def add_cross(i):
        swap(i).wait_recv()
        acc_x[...] += dot(turned[i], other_a[span(i, CHUNK), :], 1, 0, None)

    @pl.loop(0, chunks)
    def _(i):
        add_cross(i)

    cross = acc_x[...]
    cross = jnp.where(core == 0, cross, cross.T).astype(out_x.dtype)
    wide = cross.shape[1] // 2
    out_x[0] = cross[:, :wide].reshape(out_x.shape[1:])
    out_x[1] = cross[:, wide:].reshape(out_x.shape[1:])

    @pl.loop(0, spaces - 1)
    def _(i):
        to = away(i)
        for to_core in range(2):
            send(out_x.at[to_core, to], in_x.at[2 * i + core], 1, to_core, to)

    send(out_x.at[1 - core, space], in_x.at[peers - 2], 1, 1 - core, space)

    landed(in_own, recv_sems.at[0])
    mine = acc[span(space, 16), :]
    diag_ref[core, space] = mine + jnp.sum(in_own[...].astype(jnp.float32), axis=0)

    @pl.loop(0, spaces - 1)
    def _(i):
        send(diag_ref.at[core, space], diag_ref.at[core, space], 2, core, away(i))

    landed(in_x, recv_sems.at[1])
    mine = out_x[core, space].astype(jnp.float32)
    cross_ref[me] = mine + jnp.sum(in_x[...].astype(jnp.float32), axis=0)

    @pl.loop(0, spaces - 1)
    def _(i):
        to = away(i)
        for to_core in range(2):
            send(cross_ref.at[me], cross_ref.at[me], 3, to_core, to)

    send(cross_ref.at[me], cross_ref.at[me], 3, 1 - core, space)

    landed(diag_ref.at[0, pl.ds(0, spaces - 1)], recv_sems.at[2])
    send(diag_ref.at[core], diag_ref.at[core], 4, 1 - core, space)
    landed(cross_ref.at[pl.ds(0, peers - 1)], recv_sems.at[3])
    landed(in_own, send_sems.at[0])
    landed(in_x, send_sems.at[1])
    landed(diag_ref.at[0, pl.ds(0, spaces - 1)], send_sems.at[2])
    landed(cross_ref.at[pl.ds(0, peers - 1)], send_sems.at[3])

    @pl.loop(0, chunks)
    def _(i):
        swap(i).wait_send()

    for sems in (recv_sems, send_sems):
        landed(diag_ref.at[0], sems.at[4])


def subspace_kernel(points, diag_ref, cross_ref, sketch_ref, q_ref, corr_ref, gram):
    k = corr_ref.shape[0]
    cross = cross_ref[...].reshape(k // 16, 2, 16, k // 2)
    corner = jnp.concatenate([cross[:, c].reshape(k, k // 2) for c in range(2)], axis=1)
    gram[:k, :k] = diag_ref[0].reshape(k, k)
    gram[k:, k:] = diag_ref[1].reshape(k, k)
    gram[:k, k:] = corner
    gram[k:, :k] = corner.T
    block = sketch_ref[...].T
    for _ in range(ITERS):
        y = dot(block, gram[...], 1, 0)
        block = dot(inverse_factor(dot(y, y, 1, 1)), y, 1, 0)
    q_b = block.T.astype(jnp.bfloat16)
    q_ref[...] = q_b
    own = pl.multiple_of(lax.rem(lax.axis_index("leaf"), 2) * k, k)
    corr_ref[...] = dot(gram[pl.ds(own, k), :], q_b.astype(jnp.float32), 1, 0) * (1.0 / points)


def fresh_kernel(own_a, own_b, other_a, other_b, q_ref, fresh_ref, held, sem):
    core = lax.rem(lax.axis_index("leaf"), 2)
    half, k = own_a.shape
    own = pl.ds(pl.multiple_of(core * k, k), k)
    rest = pl.ds(pl.multiple_of((1 - core) * k, k), k)
    weights = jnp.concatenate([q_ref[own, :], q_ref[rest, :]], axis=0)
    copies = []
    for part, (mine, other) in enumerate(((own_a, other_b), (own_b, other_a))):
        start = (1 - core if part == 0 else core) * half
        for i in range(half // TILE):
            rows = pl.ds(i * TILE, TILE)
            at = pl.ds(part * half + i * TILE, TILE)
            merged = jnp.concatenate([mine[rows, :], other[rows, :]], axis=1)
            held[at, :] = dot(merged, weights, 1, 0, None).astype(jnp.bfloat16)
            to = fresh_ref.at[0, pl.ds(pl.multiple_of(start + i * TILE, TILE), TILE)]
            copies.append(pltpu.make_async_copy(held.at[at], to, sem.at[len(copies)]))
            copies[-1].start()
    for copy in copies:
        copy.wait()


def from_partner(value, axis, stride):
    return lax.ppermute(value, axis, [(i, i ^ 1 << stride) for i in range(lax.axis_size(axis))])


def on_device(basis, sing_vals, sketch):
    rows, k = basis.shape[1:]
    spaces = lax.axis_size("space")
    points = rows * spaces
    half = rows // 2
    vmem = pl.BlockSpec(memory_space=pltpu.VMEM)
    any_space = pl.BlockSpec(memory_space=pl.ANY)
    f32, wire = jnp.float32, jnp.bfloat16
    chunks = half // CHUNK
    own_a, own_b, other_a, diag, cross = pl.pallas_call(
        exchange_kernel,
        out_shape=(
            pltpu.VMEM((half, k), jnp.bfloat16),
            pltpu.VMEM((half, k), jnp.bfloat16),
            pltpu.VMEM((half, k), jnp.bfloat16),
            pltpu.VMEM((2, spaces, k // spaces, k), f32),
            pltpu.VMEM((2 * spaces, k // spaces, k // 2), f32),
        ),
        in_specs=[pl.BlockSpec(memory_space=pltpu.HBM)] * 2,
        out_specs=(vmem,) * 5,
        scratch_shapes=[
            pltpu.VMEM((1, k), f32),
            pltpu.VMEM((chunks, k, CHUNK), jnp.bfloat16),
            pltpu.VMEM((k, k), f32),
            pltpu.VMEM((k, k), f32),
            pltpu.VMEM((spaces, k // spaces, k), wire),
            pltpu.VMEM((spaces - 1, k // spaces, k), wire),
            pltpu.VMEM((2, spaces, k // spaces, k // 2), wire),
            pltpu.VMEM((2 * spaces - 1, k // spaces, k // 2), wire),
            pltpu.SemaphoreType.REGULAR,
            pltpu.SemaphoreType.REGULAR,
            pltpu.SemaphoreType.DMA,
            pltpu.SemaphoreType.DMA((chunks + half // STRIP,)),
            pltpu.SemaphoreType.DMA((chunks,)),
            pltpu.SemaphoreType.DMA((chunks,)),
            pltpu.SemaphoreType.DMA((5,)),
            pltpu.SemaphoreType.DMA((5,)),
        ],
        compiler_params=pltpu.CompilerParams(
            collective_id=0, has_side_effects=True, vmem_limit_bytes=36 * 2**20
        ),
        name="exchange",
    )(basis, sing_vals)
    other_b = from_partner(own_b, "leaf", 0)
    block_b, correlation = pl.pallas_call(
        functools.partial(subspace_kernel, points),
        out_shape=(
            jax.ShapeDtypeStruct(sketch.shape, jnp.bfloat16),
            jax.ShapeDtypeStruct((k, k), f32),
        ),
        in_specs=[vmem, vmem, vmem],
        out_specs=(vmem, vmem),
        scratch_shapes=[pltpu.VMEM((2 * k, 2 * k), f32)],
        compiler_params=pltpu.CompilerParams(vmem_limit_bytes=16 * 2**20),
        cost_estimate=pl.CostEstimate(flops=2**31, bytes_accessed=80 * 2**20, transcendentals=0),
        name="subspace",
    )(diag, cross, sketch)
    fresh = pl.pallas_call(
        fresh_kernel,
        out_shape=jax.ShapeDtypeStruct((1, rows, k), jnp.bfloat16),
        in_specs=[vmem] * 5,
        out_specs=any_space,
        scratch_shapes=[
            pltpu.VMEM((rows, k), jnp.bfloat16),
            pltpu.SemaphoreType.DMA((rows // TILE,)),
        ],
        compiler_params=pltpu.CompilerParams(vmem_limit_bytes=32 * 2**20),
        name="fresh",
    )(own_a, own_b, other_a, other_b, block_b)
    return (fresh, correlation[None])


def solution(mesh):
    in_specs = (P("leaf", "space", None), P("leaf", None), P())
    out_specs = (P("leaf", "space", None), P("leaf", None, None))
    return jax.shard_map(
        on_device, mesh=mesh, in_specs=in_specs, out_specs=out_specs, check_vma=False
    )
```

```python
import functools
import jax
import jax.numpy as jnp
from jax import lax
from jax.experimental import pallas as pl
from jax.experimental.pallas import tpu as pltpu
from jax.sharding import PartitionSpec as P

ITERS = 2
PANEL = 32
SUB = 16
CHUNK = 1024
STRIP = 2048
TILE = 512
MESH = pl.DeviceIdType.MESH
EXACT = lax.Precision.HIGH


def dot(a, b, on_a, on_b, precision=EXACT):
    dims = (((on_a,), (on_b,)), ((), ()))
    return lax.dot_general(a, b, dims, precision=precision, preferred_element_type=jnp.float32)


def stack(block):
    terms = []
    for _ in range(3):
        terms.append(block.astype(jnp.bfloat16))
        block = block - terms[-1].astype(jnp.float32)
    high, mid, low = terms
    left = jnp.concatenate([high, mid, high, mid, low, high], axis=0)
    return left, jnp.concatenate([high, high, mid, mid, high, low], axis=0)


def inverse_factor(inner):
    n = inner.shape[0]
    count = n // PANEL
    tile = (8, 128)
    tall, wide = PANEL // 8, n // 128
    lane = lax.broadcasted_iota(jnp.int32, tile, 1)
    row = lax.broadcasted_iota(jnp.int32, tile, 0)
    lane_wide = lax.broadcasted_iota(jnp.int32, (PANEL, n), 1)
    unit = [jnp.where(row == s, 1.0, 0.0) for s in range(8)]
    panels = [inner[i * PANEL : (i + 1) * PANEL] for i in range(count)]
    done = []
    for p in range(count):
        first = p * PANEL
        here, base = first // 128, first % 128
        w = [
            [panels[p][8 * r : 8 * r + 8, 128 * h : 128 * h + 128] for h in range(wide)]
            for r in range(tall)
        ]
        diag = [jnp.zeros(tile, jnp.float32)] * tall
        for sub in range(0, PANEL, SUB):
            cols = [
                {
                    r: jnp.broadcast_to(w[r][here][:, base + sub + j : base + sub + j + 1], tile)
                    for r in range(sub // 8, tall)
                }
                for j in range(SUB)
            ]
            for j in range(SUB):
                at = sub + j
                top, s = at // 8, at % 8
                inv = 1.0 / jnp.broadcast_to(cols[j][top][s : s + 1], tile)
                mult = {r: cols[j][r] * inv for r in range(top, tall)}
                mult[top] = jnp.where(row > s, mult[top], 0.0)
                if s == 7:
                    del mult[top]
                for k in range(j + 1, SUB):
                    pivot = cols[k][top][s : s + 1]
                    for r in mult:
                        cols[k][r] = cols[k][r] - mult[r] * pivot
                diag[top] = jnp.where(row == s, cols[j][top], diag[top])
                at_lane = lane == base + at
                w[top][here] = jnp.where(at_lane, unit[s], w[top][here])
                for r in range(top + 1, tall):
                    w[r][here] = jnp.where(at_lane, 0.0, w[r][here])
                for h in range(wide):
                    pivot = w[top][h][s : s + 1]
                    for r in mult:
                        w[r][h] = w[r][h] - mult[r] * pivot
        for r in range(tall):
            scale = lax.rsqrt(diag[r])
            w[r] = [value * scale for value in w[r]]
            if r + 1 < tall:
                above = (lane >= base + 8 * r + 8) & (lane < base + PANEL)
                w[r][here] = jnp.where(above, 0.0, w[r][here])
        block = jnp.concatenate([jnp.concatenate(tiles, axis=1) for tiles in w], axis=0)
        after = first + PANEL
        if after == n:
            done.append(block)
            break
        done.append(jnp.where(lane_wide < after, block, 0.0))
        blank = (lane_wide >= first) & (lane_wide < after)
        left, right = stack(block)
        turned = [left[:, 128 * h : 128 * h + 128].T for h in range(wide)]
        near = dot(turned[after // 128][after % 128 : after % 128 + PANEL], right, 1, 0, None)
        panels[p + 1] = jnp.where(blank, 0.0, panels[p + 1]) - near
        if after + PANEL < n:
            far = dot(jnp.concatenate(turned, axis=0)[after + PANEL :], right, 1, 0, None)
            for m in range(p + 2, count):
                at = (m - p - 2) * PANEL
                panels[m] = jnp.where(blank, 0.0, panels[m]) - far[at : at + PANEL]
    return jnp.concatenate(done, axis=0)


def exchange_kernel(
    basis_ref, sing_ref, own_a, own_b, other_a, other_b, diag_ref, cross_ref,
    turned, acc, acc_x, out_own, in_own, out_x, in_x,
    answer, entered, load_sem, swap_send, swap_recv, rest_sems, send_sems, recv_sems,
):
    leaf, space = lax.axis_index("leaf"), lax.axis_index("space")
    spaces = lax.axis_size("space")
    peers = 2 * spaces
    core, pair = lax.rem(leaf, 2), lax.div(leaf, 2)
    me = space * 2 + core
    partner = (leaf + 1 - 2 * core, space)
    half = own_a.shape[0]
    chunks, strips = half // CHUNK, half // STRIP

    def away(i):
        side = 4
        k, m = lax.div(i, side), lax.rem(i, side)
        dy = lax.rem(2 + k + lax.div(k, 2) * (5 - 2 * k), side)
        dz = lax.rem(2 + m + lax.div(m, 2) * (5 - 2 * m), side)
        y, z = lax.div(space, side), lax.rem(space, side)
        return lax.rem(y + dy, side) * side + lax.rem(z + dz, side)

    def span(i, size, start=0):
        return pl.ds(pl.multiple_of(start + i * size, size), size)

    def load(part, start, i, size, sem):
        return pltpu.make_async_copy(
            basis_ref.at[0, span(i, size, start)], part.at[span(i, size)], sem
        )

    def scale(part, i, size):
        rows = span(i, size)
        part[rows, :] = (part[rows, :].astype(jnp.float32) * sing_ref[...]).astype(jnp.bfloat16)

    def swap(i):
        return pltpu.make_async_remote_copy(
            src_ref=own_a.at[span(i, CHUNK)], dst_ref=other_a.at[span(i, CHUNK)],
            send_sem=swap_send.at[i], recv_sem=swap_recv.at[i],
            device_id=partner, device_id_type=MESH,
        )

    swap_rest = pltpu.make_async_remote_copy(
        src_ref=own_b, dst_ref=other_b, send_sem=rest_sems.at[0], recv_sem=rest_sems.at[1],
        device_id=partner, device_id_type=MESH,
    )

    def send(src, dst, which, to_core, to_space):
        pltpu.make_async_remote_copy(
            src_ref=src, dst_ref=dst, send_sem=send_sems.at[which], recv_sem=recv_sems.at[which],
            device_id=(pair * 2 + to_core, to_space), device_id_type=MESH,
        ).start()

    def landed(ref, sem):
        pltpu.make_async_copy(ref, ref, sem).wait()

    first, second = (1 - core) * half, core * half
    for i in range(chunks):
        load(own_a, first, i, CHUNK, load_sem.at[i]).start()
    for i in range(strips):
        load(own_b, second, i, STRIP, load_sem.at[chunks + i]).start()

    barrier = pltpu.get_barrier_semaphore()

    @pl.when(core == 1)
    def _():
        pl.semaphore_signal(barrier, inc=1, device_id=partner, device_id_type=MESH)

    @pl.when(core == 0)
    def _():
        pl.semaphore_wait(barrier, 1)
        pl.semaphore_signal(answer, inc=1, device_id=partner, device_id_type=MESH)

    @pl.when(core == 1)
    def _():
        pl.semaphore_wait(answer, 1)

        @pl.loop(0, spaces - 1)
        def _(i):
            pl.semaphore_signal(
                barrier, inc=1, device_id=(leaf, away(i)), device_id_type=MESH
            )

    acc[...] = jnp.zeros_like(acc)
    acc_x[...] = jnp.zeros_like(acc_x)
    load(own_a, first, 0, CHUNK, load_sem.at[0]).wait()
    scale(own_a, 0, CHUNK)
    swap(0).start()

    @pl.loop(1, chunks)
    def _(i):
        load(own_a, first, i, CHUNK, load_sem.at[i]).wait()
        scale(own_a, i, CHUNK)
        swap(i).start()

    @pl.loop(0, strips)
    def _(i):
        value = own_a[span(i, STRIP), :]
        acc[...] += dot(value, value, 0, 0, None)

    @pl.loop(0, strips)
    def _(i):
        load(own_b, second, i, STRIP, load_sem.at[chunks + i]).wait()
        scale(own_b, i, STRIP)
        value = own_b[span(i, STRIP), :]
        flipped = value.T
        for part in range(STRIP // CHUNK):
            turned[i * (STRIP // CHUNK) + part] = flipped[:, part * CHUNK : (part + 1) * CHUNK]
        acc[...] += dot(flipped, value, 1, 0, None)

    @pl.when(core == 1)
    def _():
        pl.semaphore_wait(barrier, spaces - 1)
        pl.semaphore_signal(entered, inc=1, device_id=partner, device_id_type=MESH)

    @pl.when(core == 0)
    def _():
        pl.semaphore_wait(entered, 1)

    out_own[...] = acc[...].astype(out_own.dtype).reshape(out_own.shape)

    @pl.loop(0, spaces - 1)
    def _(i):
        to = away(i)
        send(out_own.at[to], in_own.at[i], 0, core, to)

    def add_cross(i):
        swap(i).wait_recv()
        acc_x[...] += dot(turned[i], other_a[span(i, CHUNK), :], 1, 0, None)

    @pl.loop(0, chunks)
    def _(i):
        add_cross(i)

    cross = acc_x[...].astype(out_x.dtype)
    cross = jnp.where(core == 0, cross, cross.T)
    wide = cross.shape[1] // 2
    out_x[0] = cross[:, :wide].reshape(out_x.shape[1:])
    out_x[1] = cross[:, wide:].reshape(out_x.shape[1:])

    @pl.loop(0, spaces - 1)
    def _(i):
        to = away(i)
        for to_core in range(2):
            send(out_x.at[to_core, to], in_x.at[2 * i + core], 1, to_core, to)

    send(out_x.at[1 - core, space], in_x.at[peers - 2], 1, 1 - core, space)

    swap_rest.start()

    landed(in_own, recv_sems.at[0])
    mine = acc[span(space, 16), :]
    diag_ref[core, space] = mine + jnp.sum(in_own[...].astype(jnp.float32), axis=0)

    @pl.loop(0, spaces - 1)
    def _(i):
        send(diag_ref.at[core, space], diag_ref.at[core, space], 2, core, away(i))

    landed(in_x, recv_sems.at[1])
    mine = out_x[core, space].astype(jnp.float32)
    total = mine + jnp.sum(in_x[...].astype(jnp.float32), axis=0)
    cross_ref[me] = total.astype(cross_ref.dtype)

    @pl.loop(0, spaces - 1)
    def _(i):
        to = away(i)
        for to_core in range(2):
            send(cross_ref.at[me], cross_ref.at[me], 3, to_core, to)

    send(cross_ref.at[me], cross_ref.at[me], 3, 1 - core, space)

    landed(diag_ref.at[0, pl.ds(0, spaces - 1)], recv_sems.at[2])
    send(diag_ref.at[core], diag_ref.at[core], 4, 1 - core, space)
    landed(cross_ref.at[pl.ds(0, peers - 1)], recv_sems.at[3])
    landed(in_own, send_sems.at[0])
    landed(in_x, send_sems.at[1])
    landed(diag_ref.at[0, pl.ds(0, spaces - 1)], send_sems.at[2])
    landed(cross_ref.at[pl.ds(0, peers - 1)], send_sems.at[3])

    @pl.loop(0, chunks)
    def _(i):
        swap(i).wait_send()

    swap_rest.wait()
    for sems in (recv_sems, send_sems):
        landed(diag_ref.at[0], sems.at[4])


def subspace_kernel(points, diag_ref, cross_ref, sketch_ref, q_ref, corr_ref, gram):
    k = corr_ref.shape[0]
    cross = cross_ref[...].astype(jnp.float32).reshape(k // 16, 2, 16, k // 2)
    corner = jnp.concatenate([cross[:, c].reshape(k, k // 2) for c in range(2)], axis=1)
    gram[:k, :k] = diag_ref[0].reshape(k, k)
    gram[k:, k:] = diag_ref[1].reshape(k, k)
    gram[:k, k:] = corner
    gram[k:, :k] = corner.T
    block = sketch_ref[...].T
    for _ in range(ITERS):
        y = dot(block, gram[...], 1, 0)
        block = dot(inverse_factor(dot(y, y, 1, 1)), y, 1, 0)
    q_b = block.T.astype(jnp.bfloat16)
    q_ref[...] = q_b
    own = pl.multiple_of(lax.rem(lax.axis_index("leaf"), 2) * k, k)
    corr_ref[...] = dot(gram[pl.ds(own, k), :], q_b.astype(jnp.float32), 1, 0) * (1.0 / points)


def fresh_kernel(own_a, own_b, other_a, other_b, q_ref, fresh_ref, held, sem):
    core = lax.rem(lax.axis_index("leaf"), 2)
    half, k = own_a.shape
    own = pl.ds(pl.multiple_of(core * k, k), k)
    rest = pl.ds(pl.multiple_of((1 - core) * k, k), k)
    weights = jnp.concatenate([q_ref[own, :], q_ref[rest, :]], axis=0)
    copies = []
    for part, (mine, other) in enumerate(((own_a, other_b), (own_b, other_a))):
        start = (1 - core if part == 0 else core) * half
        for i in range(half // TILE):
            rows = pl.ds(i * TILE, TILE)
            at = pl.ds(part * half + i * TILE, TILE)
            merged = jnp.concatenate([mine[rows, :], other[rows, :]], axis=1)
            held[at, :] = dot(merged, weights, 1, 0, None).astype(jnp.bfloat16)
            to = fresh_ref.at[0, pl.ds(pl.multiple_of(start + i * TILE, TILE), TILE)]
            copies.append(pltpu.make_async_copy(held.at[at], to, sem.at[len(copies)]))
            copies[-1].start()
    for copy in copies:
        copy.wait()


def on_device(basis, sing_vals, sketch):
    rows, k = basis.shape[1:]
    spaces = lax.axis_size("space")
    points = rows * spaces
    half = rows // 2
    vmem = pl.BlockSpec(memory_space=pltpu.VMEM)
    any_space = pl.BlockSpec(memory_space=pl.ANY)
    f32, wire = jnp.float32, jnp.bfloat16
    chunks = half // CHUNK
    own_a, own_b, other_a, other_b, diag, cross = pl.pallas_call(
        exchange_kernel,
        out_shape=(
            pltpu.VMEM((half, k), jnp.bfloat16),
            pltpu.VMEM((half, k), jnp.bfloat16),
            pltpu.VMEM((half, k), jnp.bfloat16),
            pltpu.VMEM((half, k), jnp.bfloat16),
            pltpu.VMEM((2, spaces, k // spaces, k), f32),
            pltpu.VMEM((2 * spaces, k // spaces, k // 2), wire),
        ),
        in_specs=[pl.BlockSpec(memory_space=pltpu.HBM), vmem],
        out_specs=(vmem,) * 6,
        scratch_shapes=[
            pltpu.VMEM((chunks, k, CHUNK), jnp.bfloat16),
            pltpu.VMEM((k, k), f32),
            pltpu.VMEM((k, k), f32),
            pltpu.VMEM((spaces, k // spaces, k), wire),
            pltpu.VMEM((spaces - 1, k // spaces, k), wire),
            pltpu.VMEM((2, spaces, k // spaces, k // 2), wire),
            pltpu.VMEM((2 * spaces - 1, k // spaces, k // 2), wire),
            pltpu.SemaphoreType.REGULAR,
            pltpu.SemaphoreType.REGULAR,
            pltpu.SemaphoreType.DMA((chunks + half // STRIP,)),
            pltpu.SemaphoreType.DMA((chunks,)),
            pltpu.SemaphoreType.DMA((chunks,)),
            pltpu.SemaphoreType.DMA((2,)),
            pltpu.SemaphoreType.DMA((5,)),
            pltpu.SemaphoreType.DMA((5,)),
        ],
        compiler_params=pltpu.CompilerParams(
            collective_id=0, has_side_effects=True, vmem_limit_bytes=36 * 2**20
        ),
        name="exchange",
    )(basis, sing_vals)
    block_b, correlation = pl.pallas_call(
        functools.partial(subspace_kernel, points),
        out_shape=(
            jax.ShapeDtypeStruct(sketch.shape, jnp.bfloat16),
            jax.ShapeDtypeStruct((k, k), f32),
        ),
        in_specs=[vmem, vmem, vmem],
        out_specs=(vmem, vmem),
        scratch_shapes=[pltpu.VMEM((2 * k, 2 * k), f32)],
        compiler_params=pltpu.CompilerParams(vmem_limit_bytes=16 * 2**20),
        cost_estimate=pl.CostEstimate(flops=2**31, bytes_accessed=80 * 2**20, transcendentals=0),
        name="subspace",
    )(diag, cross, sketch)
    fresh = pl.pallas_call(
        fresh_kernel,
        out_shape=jax.ShapeDtypeStruct((1, rows, k), jnp.bfloat16),
        in_specs=[vmem] * 5,
        out_specs=any_space,
        scratch_shapes=[
            pltpu.VMEM((rows, k), jnp.bfloat16),
            pltpu.SemaphoreType.DMA((rows // TILE,)),
        ],
        compiler_params=pltpu.CompilerParams(vmem_limit_bytes=32 * 2**20),
        name="fresh",
    )(own_a, own_b, other_a, other_b, block_b)
    return (fresh, correlation[None])


def solution(mesh):
    in_specs = (P("leaf", "space", None), P("leaf", None), P())
    out_specs = (P("leaf", "space", None), P("leaf", None, None))
    return jax.shard_map(
        on_device, mesh=mesh, in_specs=in_specs, out_specs=out_specs, check_vma=False
    )
```

```python
import functools
import jax
import jax.numpy as jnp
from jax import lax
from jax.experimental import pallas as pl
from jax.experimental.pallas import tpu as pltpu
from jax.sharding import PartitionSpec as P

ITERS = 2
PANEL = 32
SUB = 16
CHUNK = 2048
STRIP = 4096
TILE = 512
MESH = pl.DeviceIdType.MESH
EXACT = lax.Precision.HIGH


def dot(a, b, on_a, on_b, precision=EXACT):
    dims = (((on_a,), (on_b,)), ((), ()))
    return lax.dot_general(a, b, dims, precision=precision, preferred_element_type=jnp.float32)


def stack(block):
    terms = []
    for _ in range(3):
        terms.append(block.astype(jnp.bfloat16))
        block = block - terms[-1].astype(jnp.float32)
    high, mid, low = terms
    left = jnp.concatenate([high, mid, high, mid, low, high], axis=0)
    return left, jnp.concatenate([high, high, mid, mid, high, low], axis=0)


def inverse_factor(inner):
    n = inner.shape[0]
    count = n // PANEL
    tile = (8, 128)
    tall, wide = PANEL // 8, n // 128
    lane = lax.broadcasted_iota(jnp.int32, tile, 1)
    row = lax.broadcasted_iota(jnp.int32, tile, 0)
    lane_wide = lax.broadcasted_iota(jnp.int32, (PANEL, n), 1)
    unit = [jnp.where(row == s, 1.0, 0.0) for s in range(8)]
    shrink, grow = [], []
    for h in range(wide):
        corner = inner[128 * h : 128 * h + 128, 128 * h : 128 * h + 128]
        square = [lax.broadcasted_iota(jnp.int32, (128, 128), axis) for axis in range(2)]
        spots = jnp.sum(jnp.where(square[0] == square[1], corner, 0.0), axis=0, keepdims=True)
        spots = jnp.broadcast_to(spots, tile)
        shrink.append(lax.rsqrt(spots))
        grow.append(spots * shrink[h])
    panels = [inner[i * PANEL : (i + 1) * PANEL] for i in range(count)]
    done = []
    for p in range(count):
        first = p * PANEL
        here, base = first // 128, first % 128
        w = [
            [panels[p][8 * r : 8 * r + 8, 128 * h : 128 * h + 128] for h in range(wide)]
            for r in range(tall)
        ]
        diag = [jnp.zeros(tile, jnp.float32)] * tall
        for sub in range(0, PANEL, SUB):
            near_cols = {r: w[r][here] * shrink[here] for r in range(sub // 8, tall)}
            spots = [base + sub + j for j in range(SUB)]
            cols = [
                {r: jnp.broadcast_to(value[:, at : at + 1], tile) for r, value in near_cols.items()}
                for at in spots
            ]
            back = [jnp.broadcast_to(grow[here][:, at : at + 1], tile) for at in spots]
            for j in range(0, SUB, 2):
                at = sub + j
                top, s = at // 8, at % 8
                one, two = cols[j], cols[j + 1]
                a, b = (jnp.broadcast_to(one[top][s + t : s + t + 1], tile) for t in range(2))
                c, d = (jnp.broadcast_to(two[top][s + t : s + t + 1], tile) for t in range(2))
                det = a * d - b * c
                inv_det, inv_a = 1.0 / det, 1.0 / a
                left = {r: (d * one[r] - b * two[r]) * inv_det for r in range(top, tall)}
                right = {r: (a * two[r] - c * one[r]) * inv_det for r in range(top, tall)}
                left[top] = jnp.where(row > s + 1, left[top], 0.0)
                right[top] = jnp.where(row > s + 1, right[top], 0.0)
                if s == 6:
                    del left[top], right[top]
                for k in range(j + 2, SUB):
                    e, f = cols[k][top][s : s + 1], cols[k][top][s + 1 : s + 2]
                    for r in left:
                        cols[k][r] = (cols[k][r] - left[r] * e) - right[r] * f
                diag[top] = jnp.where(row == s, a * back[j], diag[top])
                diag[top] = jnp.where(row == s + 1, det * inv_a * back[j + 1], diag[top])
                for t in range(2):
                    at_lane = lane == base + at + t
                    w[top][here] = jnp.where(at_lane, unit[s + t], w[top][here])
                    for r in range(top + 1, tall):
                        w[r][here] = jnp.where(at_lane, 0.0, w[r][here])
                low = jnp.where(row == s + 1, b * inv_a, 0.0)
                for h in range(wide):
                    e, f = w[top][h][s : s + 1], w[top][h][s + 1 : s + 2]
                    for r in left:
                        w[r][h] = (w[r][h] - left[r] * e) - right[r] * f
                    w[top][h] = w[top][h] - low * e
        for r in range(tall):
            scale = lax.rsqrt(diag[r])
            w[r] = [value * scale for value in w[r]]
            if r + 1 < tall:
                above = (lane >= base + 8 * r + 8) & (lane < base + PANEL)
                w[r][here] = jnp.where(above, 0.0, w[r][here])
        block = jnp.concatenate([jnp.concatenate(tiles, axis=1) for tiles in w], axis=0)
        after = first + PANEL
        if after == n:
            done.append(block)
            break
        done.append(jnp.where(lane_wide < after, block, 0.0))
        blank = (lane_wide >= first) & (lane_wide < after)
        stacked, terms = stack(block)
        turned = [stacked[:, 128 * h : 128 * h + 128].T for h in range(wide)]
        near = dot(turned[after // 128][after % 128 : after % 128 + PANEL], terms, 1, 0, None)
        panels[p + 1] = jnp.where(blank, 0.0, panels[p + 1]) - near
        if after + PANEL < n:
            far = dot(jnp.concatenate(turned, axis=0)[after + PANEL :], terms, 1, 0, None)
            for m in range(p + 2, count):
                at = (m - p - 2) * PANEL
                panels[m] = jnp.where(blank, 0.0, panels[m]) - far[at : at + PANEL]
    return jnp.concatenate(done, axis=0)


def exchange_kernel(
    basis_ref, sing_ref, own_a, own_b, other_a, other_b, diag_ref, cross_ref,
    turned, acc, acc_x, out_own, in_own, out_x, in_x,
    answer, entered, load_sem, swap_send, swap_recv, rest_sems, send_sems, recv_sems,
):
    leaf, space = lax.axis_index("leaf"), lax.axis_index("space")
    spaces = lax.axis_size("space")
    peers = 2 * spaces
    core, pair = lax.rem(leaf, 2), lax.div(leaf, 2)
    me = space * 2 + core
    partner = (leaf + 1 - 2 * core, space)
    half = own_a.shape[0]
    chunks, strips = half // CHUNK, half // STRIP

    def away(i):
        side = 4
        k, m = lax.div(i, side), lax.rem(i, side)
        dy = lax.rem(2 + k + lax.div(k, 2) * (5 - 2 * k), side)
        dz = lax.rem(2 + m + lax.div(m, 2) * (5 - 2 * m), side)
        y, z = lax.div(space, side), lax.rem(space, side)
        return lax.rem(y + dy, side) * side + lax.rem(z + dz, side)

    def span(i, size, start=0):
        return pl.ds(pl.multiple_of(start + i * size, size), size)

    def load(part, start, i, size, sem):
        return pltpu.make_async_copy(
            basis_ref.at[0, span(i, size, start)], part.at[span(i, size)], sem
        )

    def scale(part, i, size):
        rows = span(i, size)
        part[rows, :] = (part[rows, :].astype(jnp.float32) * sing_ref[...]).astype(jnp.bfloat16)

    def swap(i):
        return pltpu.make_async_remote_copy(
            src_ref=own_a.at[span(i, CHUNK)], dst_ref=other_a.at[span(i, CHUNK)],
            send_sem=swap_send.at[i], recv_sem=swap_recv.at[i],
            device_id=partner, device_id_type=MESH,
        )

    swap_rest = pltpu.make_async_remote_copy(
        src_ref=own_b, dst_ref=other_b, send_sem=rest_sems.at[0], recv_sem=rest_sems.at[1],
        device_id=partner, device_id_type=MESH,
    )

    def send(src, dst, which, to_core, to_space):
        pltpu.make_async_remote_copy(
            src_ref=src, dst_ref=dst, send_sem=send_sems.at[which], recv_sem=recv_sems.at[which],
            device_id=(pair * 2 + to_core, to_space), device_id_type=MESH,
        ).start()

    def landed(ref, sem):
        pltpu.make_async_copy(ref, ref, sem).wait()

    first, second = (1 - core) * half, core * half
    for i in range(chunks):
        load(own_a, first, i, CHUNK, load_sem.at[i]).start()
    for i in range(strips):
        load(own_b, second, i, STRIP, load_sem.at[chunks + i]).start()

    barrier = pltpu.get_barrier_semaphore()

    @pl.when(core == 1)
    def _():
        pl.semaphore_signal(barrier, inc=1, device_id=partner, device_id_type=MESH)

    @pl.when(core == 0)
    def _():
        pl.semaphore_wait(barrier, 1)
        pl.semaphore_signal(answer, inc=1, device_id=partner, device_id_type=MESH)

    @pl.when(core == 1)
    def _():
        pl.semaphore_wait(answer, 1)

        @pl.loop(0, spaces - 1)
        def _(i):
            pl.semaphore_signal(
                barrier, inc=1, device_id=(leaf, away(i)), device_id_type=MESH
            )

    acc[...] = jnp.zeros_like(acc)
    acc_x[...] = jnp.zeros_like(acc_x)
    load(own_a, first, 0, CHUNK, load_sem.at[0]).wait()
    scale(own_a, 0, CHUNK)
    swap(0).start()

    @pl.loop(1, chunks)
    def _(i):
        load(own_a, first, i, CHUNK, load_sem.at[i]).wait()
        scale(own_a, i, CHUNK)
        swap(i).start()

    @pl.loop(0, strips)
    def _(i):
        value = own_a[span(i, STRIP), :]
        acc[...] += dot(value, value, 0, 0, None)

    @pl.loop(0, strips)
    def _(i):
        load(own_b, second, i, STRIP, load_sem.at[chunks + i]).wait()
        scale(own_b, i, STRIP)
        value = own_b[span(i, STRIP), :]
        flipped = value.T
        for part in range(STRIP // CHUNK):
            turned[i * (STRIP // CHUNK) + part] = flipped[:, part * CHUNK : (part + 1) * CHUNK]
        acc[...] += dot(flipped, value, 1, 0, None)

    @pl.when(core == 1)
    def _():
        pl.semaphore_wait(barrier, spaces - 1)
        pl.semaphore_signal(entered, inc=1, device_id=partner, device_id_type=MESH)

    @pl.when(core == 0)
    def _():
        pl.semaphore_wait(entered, 1)

    out_own[...] = acc[...].astype(out_own.dtype).reshape(out_own.shape)

    @pl.loop(0, spaces - 1)
    def _(i):
        to = away(i)
        send(out_own.at[to], in_own.at[i], 0, core, to)

    def add_cross(i):
        swap(i).wait_recv()
        acc_x[...] += dot(turned[i], other_a[span(i, CHUNK), :], 1, 0, None)

    @pl.loop(0, chunks)
    def _(i):
        add_cross(i)

    cross = acc_x[...].astype(out_x.dtype)
    cross = jnp.where(core == 0, cross, cross.T)
    wide = cross.shape[1] // 2
    out_x[0] = cross[:, :wide].reshape(out_x.shape[1:])
    out_x[1] = cross[:, wide:].reshape(out_x.shape[1:])

    @pl.loop(0, spaces - 1)
    def _(i):
        to = away(i)
        for to_core in range(2):
            send(out_x.at[to_core, to], in_x.at[2 * i + core], 1, to_core, to)

    send(out_x.at[1 - core, space], in_x.at[peers - 2], 1, 1 - core, space)

    swap_rest.start()

    landed(in_own, recv_sems.at[0])
    mine = acc[span(space, 16), :]
    diag_ref[core, space] = mine + jnp.sum(in_own[...].astype(jnp.float32), axis=0)

    @pl.loop(0, spaces - 1)
    def _(i):
        send(diag_ref.at[core, space], diag_ref.at[core, space], 2, core, away(i))

    landed(in_x, recv_sems.at[1])
    mine = out_x[core, space].astype(jnp.float32)
    total = mine + jnp.sum(in_x[...].astype(jnp.float32), axis=0)
    cross_ref[me] = total.astype(cross_ref.dtype)

    @pl.loop(0, spaces - 1)
    def _(i):
        to = away(i)
        for to_core in range(2):
            send(cross_ref.at[me], cross_ref.at[me], 3, to_core, to)

    send(cross_ref.at[me], cross_ref.at[me], 3, 1 - core, space)

    landed(diag_ref.at[0, pl.ds(0, spaces - 1)], recv_sems.at[2])
    send(diag_ref.at[core], diag_ref.at[core], 4, 1 - core, space)
    landed(cross_ref.at[pl.ds(0, peers - 1)], recv_sems.at[3])
    landed(in_own, send_sems.at[0])
    landed(in_x, send_sems.at[1])
    landed(diag_ref.at[0, pl.ds(0, spaces - 1)], send_sems.at[2])
    landed(cross_ref.at[pl.ds(0, peers - 1)], send_sems.at[3])

    @pl.loop(0, chunks)
    def _(i):
        swap(i).wait_send()

    swap_rest.wait()
    for sems in (recv_sems, send_sems):
        landed(diag_ref.at[0], sems.at[4])


def subspace_kernel(points, diag_ref, cross_ref, sketch_ref, q_ref, corr_ref, gram):
    k = corr_ref.shape[0]
    cross = cross_ref[...].astype(jnp.float32).reshape(k // 16, 2, 16, k // 2)
    corner = jnp.concatenate([cross[:, c].reshape(k, k // 2) for c in range(2)], axis=1)
    gram[:k, :k] = diag_ref[0].reshape(k, k)
    gram[k:, k:] = diag_ref[1].reshape(k, k)
    gram[:k, k:] = corner
    gram[k:, :k] = corner.T
    block = sketch_ref[...].T
    for _ in range(ITERS):
        y = dot(block, gram[...], 1, 0)
        block = dot(inverse_factor(dot(y, y, 1, 1)), y, 1, 0)
    q_b = block.T.astype(jnp.bfloat16)
    q_ref[...] = q_b
    own = pl.multiple_of(lax.rem(lax.axis_index("leaf"), 2) * k, k)
    corr_ref[...] = dot(gram[pl.ds(own, k), :], q_b.astype(jnp.float32), 1, 0) * (1.0 / points)


def fresh_kernel(own_a, own_b, other_a, other_b, q_ref, fresh_ref, held, sem):
    core = lax.rem(lax.axis_index("leaf"), 2)
    half, k = own_a.shape
    own = pl.ds(pl.multiple_of(core * k, k), k)
    rest = pl.ds(pl.multiple_of((1 - core) * k, k), k)
    weights = jnp.concatenate([q_ref[own, :], q_ref[rest, :]], axis=0)
    copies = []
    for part, (mine, other) in enumerate(((own_a, other_b), (own_b, other_a))):
        start = (1 - core if part == 0 else core) * half
        for i in range(half // TILE):
            rows = pl.ds(i * TILE, TILE)
            at = pl.ds(part * half + i * TILE, TILE)
            merged = jnp.concatenate([mine[rows, :], other[rows, :]], axis=1)
            held[at, :] = dot(merged, weights, 1, 0, None).astype(jnp.bfloat16)
            to = fresh_ref.at[0, pl.ds(pl.multiple_of(start + i * TILE, TILE), TILE)]
            copies.append(pltpu.make_async_copy(held.at[at], to, sem.at[len(copies)]))
            copies[-1].start()
    for copy in copies:
        copy.wait()


def on_device(basis, sing_vals, sketch):
    rows, k = basis.shape[1:]
    spaces = lax.axis_size("space")
    points = rows * spaces
    half = rows // 2
    vmem = pl.BlockSpec(memory_space=pltpu.VMEM)
    any_space = pl.BlockSpec(memory_space=pl.ANY)
    f32, wire = jnp.float32, jnp.bfloat16
    chunks = half // CHUNK
    own_a, own_b, other_a, other_b, diag, cross = pl.pallas_call(
        exchange_kernel,
        out_shape=(
            pltpu.VMEM((half, k), jnp.bfloat16),
            pltpu.VMEM((half, k), jnp.bfloat16),
            pltpu.VMEM((half, k), jnp.bfloat16),
            pltpu.VMEM((half, k), jnp.bfloat16),
            pltpu.VMEM((2, spaces, k // spaces, k), f32),
            pltpu.VMEM((2 * spaces, k // spaces, k // 2), wire),
        ),
        in_specs=[pl.BlockSpec(memory_space=pltpu.HBM), vmem],
        out_specs=(vmem,) * 6,
        scratch_shapes=[
            pltpu.VMEM((chunks, k, CHUNK), jnp.bfloat16),
            pltpu.VMEM((k, k), f32),
            pltpu.VMEM((k, k), f32),
            pltpu.VMEM((spaces, k // spaces, k), wire),
            pltpu.VMEM((spaces - 1, k // spaces, k), wire),
            pltpu.VMEM((2, spaces, k // spaces, k // 2), wire),
            pltpu.VMEM((2 * spaces - 1, k // spaces, k // 2), wire),
            pltpu.SemaphoreType.REGULAR,
            pltpu.SemaphoreType.REGULAR,
            pltpu.SemaphoreType.DMA((chunks + half // STRIP,)),
            pltpu.SemaphoreType.DMA((chunks,)),
            pltpu.SemaphoreType.DMA((chunks,)),
            pltpu.SemaphoreType.DMA((2,)),
            pltpu.SemaphoreType.DMA((5,)),
            pltpu.SemaphoreType.DMA((5,)),
        ],
        compiler_params=pltpu.CompilerParams(
            collective_id=0, has_side_effects=True, vmem_limit_bytes=36 * 2**20
        ),
        name="exchange",
    )(basis, sing_vals)
    block_b, correlation = pl.pallas_call(
        functools.partial(subspace_kernel, points),
        out_shape=(
            jax.ShapeDtypeStruct(sketch.shape, jnp.bfloat16),
            jax.ShapeDtypeStruct((k, k), f32),
        ),
        in_specs=[vmem, vmem, vmem],
        out_specs=(vmem, vmem),
        scratch_shapes=[pltpu.VMEM((2 * k, 2 * k), f32)],
        compiler_params=pltpu.CompilerParams(vmem_limit_bytes=16 * 2**20),
        cost_estimate=pl.CostEstimate(flops=2**31, bytes_accessed=80 * 2**20, transcendentals=0),
        name="subspace",
    )(diag, cross, sketch)
    fresh = pl.pallas_call(
        fresh_kernel,
        out_shape=jax.ShapeDtypeStruct((1, rows, k), jnp.bfloat16),
        in_specs=[vmem] * 5,
        out_specs=any_space,
        scratch_shapes=[
            pltpu.VMEM((rows, k), jnp.bfloat16),
            pltpu.SemaphoreType.DMA((rows // TILE,)),
        ],
        compiler_params=pltpu.CompilerParams(vmem_limit_bytes=32 * 2**20),
        name="fresh",
    )(own_a, own_b, other_a, other_b, block_b)
    return (fresh, correlation[None])


def solution(mesh):
    in_specs = (P("leaf", "space", None), P("leaf", None), P())
    out_specs = (P("leaf", "space", None), P("leaf", None, None))
    return jax.shard_map(
        on_device, mesh=mesh, in_specs=in_specs, out_specs=out_specs, check_vma=False
    )
```

```python
import functools
import jax
import jax.numpy as jnp
from jax import lax
from jax.experimental import pallas as pl
from jax.experimental.pallas import tpu as pltpu
from jax.sharding import PartitionSpec as P

ITERS = 2
PANEL = 32
SUB = 16
CHUNK = 2048
STRIP = 4096
TILE = 512
MESH = pl.DeviceIdType.MESH
EXACT = lax.Precision.HIGH


def dot(a, b, on_a, on_b, precision=EXACT):
    dims = (((on_a,), (on_b,)), ((), ()))
    return lax.dot_general(a, b, dims, precision=precision, preferred_element_type=jnp.float32)


def stack(block):
    terms = []
    for _ in range(3):
        terms.append(block.astype(jnp.bfloat16))
        block = block - terms[-1].astype(jnp.float32)
    high, mid, low = terms
    left = jnp.concatenate([high, mid, high, mid, low, high], axis=0)
    return left, jnp.concatenate([high, high, mid, mid, high, low], axis=0)


def inverse_factor(inner):
    n = inner.shape[0]
    count = n // PANEL
    tile = (8, 128)
    tall, wide = PANEL // 8, n // 128
    lane = lax.broadcasted_iota(jnp.int32, tile, 1)
    row = lax.broadcasted_iota(jnp.int32, tile, 0)
    lane_wide = lax.broadcasted_iota(jnp.int32, (PANEL, n), 1)
    unit = [jnp.where(row == s, 1.0, 0.0) for s in range(8)]
    shrink, grow = [], []
    for h in range(wide):
        corner = inner[128 * h : 128 * h + 128, 128 * h : 128 * h + 128]
        square = [lax.broadcasted_iota(jnp.int32, (128, 128), axis) for axis in range(2)]
        spots = jnp.sum(jnp.where(square[0] == square[1], corner, 0.0), axis=0, keepdims=True)
        spots = jnp.broadcast_to(spots, tile)
        shrink.append(lax.rsqrt(spots))
        grow.append(spots * shrink[h])
    panels = [inner[i * PANEL : (i + 1) * PANEL] for i in range(count)]
    done = []
    for p in range(count):
        first = p * PANEL
        here, base = first // 128, first % 128
        w = [
            [panels[p][8 * r : 8 * r + 8, 128 * h : 128 * h + 128] for h in range(wide)]
            for r in range(tall)
        ]
        diag = [jnp.zeros(tile, jnp.float32)] * tall
        for sub in range(0, PANEL, SUB):
            near_cols = {r: w[r][here] * shrink[here] for r in range(sub // 8, tall)}
            spots = [base + sub + j for j in range(SUB)]
            cols = [
                {r: jnp.broadcast_to(value[:, at : at + 1], tile) for r, value in near_cols.items()}
                for at in spots
            ]
            back = [jnp.broadcast_to(grow[here][:, at : at + 1], tile) for at in spots]
            for j in range(0, SUB, 2):
                at = sub + j
                top, s = at // 8, at % 8
                one, two = cols[j], cols[j + 1]
                a, b = (jnp.broadcast_to(one[top][s + t : s + t + 1], tile) for t in range(2))
                c, d = (jnp.broadcast_to(two[top][s + t : s + t + 1], tile) for t in range(2))
                det = a * d - b * c
                inv_det, inv_a = 1.0 / det, 1.0 / a
                left = {r: (d * one[r] - b * two[r]) * inv_det for r in range(top, tall)}
                right = {r: (a * two[r] - c * one[r]) * inv_det for r in range(top, tall)}
                left[top] = jnp.where(row > s + 1, left[top], 0.0)
                right[top] = jnp.where(row > s + 1, right[top], 0.0)
                if s == 6:
                    del left[top], right[top]
                for k in range(j + 2, SUB):
                    e, f = cols[k][top][s : s + 1], cols[k][top][s + 1 : s + 2]
                    for r in left:
                        cols[k][r] = (cols[k][r] - left[r] * e) - right[r] * f
                diag[top] = jnp.where(row == s, a * back[j], diag[top])
                diag[top] = jnp.where(row == s + 1, det * inv_a * back[j + 1], diag[top])
                for t in range(2):
                    at_lane = lane == base + at + t
                    w[top][here] = jnp.where(at_lane, unit[s + t], w[top][here])
                    for r in range(top + 1, tall):
                        w[r][here] = jnp.where(at_lane, 0.0, w[r][here])
                low = jnp.where(row == s + 1, b * inv_a, 0.0)
                for h in range(wide):
                    e, f = w[top][h][s : s + 1], w[top][h][s + 1 : s + 2]
                    for r in left:
                        w[r][h] = (w[r][h] - left[r] * e) - right[r] * f
                    w[top][h] = w[top][h] - low * e
        for r in range(tall):
            scale = lax.rsqrt(diag[r])
            w[r] = [value * scale for value in w[r]]
            if r + 1 < tall:
                above = (lane >= base + 8 * r + 8) & (lane < base + PANEL)
                w[r][here] = jnp.where(above, 0.0, w[r][here])
        block = jnp.concatenate([jnp.concatenate(tiles, axis=1) for tiles in w], axis=0)
        after = first + PANEL
        if after == n:
            done.append(block)
            break
        done.append(jnp.where(lane_wide < after, block, 0.0))
        blank = (lane_wide >= first) & (lane_wide < after)
        stacked, terms = stack(block)
        turned = [stacked[:, 128 * h : 128 * h + 128].T for h in range(wide)]
        near = dot(turned[after // 128][after % 128 : after % 128 + PANEL], terms, 1, 0, None)
        panels[p + 1] = jnp.where(blank, 0.0, panels[p + 1]) - near
        if after + PANEL < n:
            far = dot(jnp.concatenate(turned, axis=0)[after + PANEL :], terms, 1, 0, None)
            for m in range(p + 2, count):
                at = (m - p - 2) * PANEL
                panels[m] = jnp.where(blank, 0.0, panels[m]) - far[at : at + PANEL]
    return jnp.concatenate(done, axis=0)


def exchange_kernel(
    basis_ref, sing_ref, own_a, own_b, other_a, other_b, diag_ref, cross_ref,
    turned, acc, acc_x, out_own, in_own, out_x, in_x,
    answer, entered, load_sem, swap_send, swap_recv, rest_sems, send_sems, recv_sems,
):
    leaf, space = lax.axis_index("leaf"), lax.axis_index("space")
    spaces = lax.axis_size("space")
    peers = 2 * spaces
    core, pair = lax.rem(leaf, 2), lax.div(leaf, 2)
    me = space * 2 + core
    partner = (leaf + 1 - 2 * core, space)
    half = own_a.shape[0]
    chunks, strips = half // CHUNK, half // STRIP

    def away(i):
        side = 4
        k, m = lax.div(i, side), lax.rem(i, side)
        dy = lax.rem(2 + k + lax.div(k, 2) * (5 - 2 * k), side)
        dz = lax.rem(2 + m + lax.div(m, 2) * (5 - 2 * m), side)
        y, z = lax.div(space, side), lax.rem(space, side)
        return lax.rem(y + dy, side) * side + lax.rem(z + dz, side)

    def span(i, size, start=0):
        return pl.ds(pl.multiple_of(start + i * size, size), size)

    def load(part, start, i, size, sem):
        return pltpu.make_async_copy(
            basis_ref.at[0, span(i, size, start)], part.at[span(i, size)], sem
        )

    def scale(part, i, size):
        rows = span(i, size)
        part[rows, :] = (part[rows, :].astype(jnp.float32) * sing_ref[...]).astype(jnp.bfloat16)

    def swap(i):
        return pltpu.make_async_remote_copy(
            src_ref=own_a.at[span(i, CHUNK)], dst_ref=other_a.at[span(i, CHUNK)],
            send_sem=swap_send.at[i], recv_sem=swap_recv.at[i],
            device_id=partner, device_id_type=MESH,
        )

    swap_rest = pltpu.make_async_remote_copy(
        src_ref=own_b, dst_ref=other_b, send_sem=rest_sems.at[0], recv_sem=rest_sems.at[1],
        device_id=partner, device_id_type=MESH,
    )

    def send(src, dst, which, to_core, to_space):
        pltpu.make_async_remote_copy(
            src_ref=src, dst_ref=dst, send_sem=send_sems.at[which], recv_sem=recv_sems.at[which],
            device_id=(pair * 2 + to_core, to_space), device_id_type=MESH,
        ).start()

    def landed(ref, sem):
        pltpu.make_async_copy(ref, ref, sem).wait()

    first, second = (1 - core) * half, core * half
    for i in range(chunks):
        load(own_a, first, i, CHUNK, load_sem.at[i]).start()
    for i in range(strips):
        load(own_b, second, i, STRIP, load_sem.at[chunks + i]).start()

    barrier = pltpu.get_barrier_semaphore()

    @pl.when(core == 1)
    def _():
        pl.semaphore_signal(barrier, inc=1, device_id=partner, device_id_type=MESH)

    @pl.when(core == 0)
    def _():
        pl.semaphore_wait(barrier, 1)
        pl.semaphore_signal(answer, inc=1, device_id=partner, device_id_type=MESH)

    @pl.when(core == 1)
    def _():
        pl.semaphore_wait(answer, 1)

        @pl.loop(0, spaces - 1)
        def _(i):
            pl.semaphore_signal(
                barrier, inc=1, device_id=(leaf, away(i)), device_id_type=MESH
            )

    acc[...] = jnp.zeros_like(acc)
    acc_x[...] = jnp.zeros_like(acc_x)
    load(own_a, first, 0, CHUNK, load_sem.at[0]).wait()
    scale(own_a, 0, CHUNK)
    swap(0).start()

    @pl.loop(1, chunks)
    def _(i):
        load(own_a, first, i, CHUNK, load_sem.at[i]).wait()
        scale(own_a, i, CHUNK)
        swap(i).start()

    @pl.loop(0, strips)
    def _(i):
        value = own_a[span(i, STRIP), :]
        acc[...] += dot(value, value, 0, 0, None)

    @pl.loop(0, strips)
    def _(i):
        load(own_b, second, i, STRIP, load_sem.at[chunks + i]).wait()
        scale(own_b, i, STRIP)
        value = own_b[span(i, STRIP), :]
        flipped = value.T
        for part in range(STRIP // CHUNK):
            turned[i * (STRIP // CHUNK) + part] = flipped[:, part * CHUNK : (part + 1) * CHUNK]
        acc[...] += dot(flipped, value, 1, 0, None)

    @pl.when(core == 1)
    def _():
        pl.semaphore_wait(barrier, spaces - 1)
        pl.semaphore_signal(entered, inc=1, device_id=partner, device_id_type=MESH)

    @pl.when(core == 0)
    def _():
        pl.semaphore_wait(entered, 1)

    out_own[...] = acc[...].astype(out_own.dtype).reshape(out_own.shape)

    @pl.loop(0, spaces - 1)
    def _(i):
        to = away(i)
        send(out_own.at[to], in_own.at[i], 0, core, to)

    def add_cross(i):
        swap(i).wait_recv()
        acc_x[...] += dot(turned[i], other_a[span(i, CHUNK), :], 1, 0, None)

    @pl.loop(0, chunks)
    def _(i):
        add_cross(i)

    cross = acc_x[...].astype(out_x.dtype)
    cross = jnp.where(core == 0, cross, cross.T)
    wide = cross.shape[1] // 2
    out_x[0] = cross[:, :wide].reshape(out_x.shape[1:])
    out_x[1] = cross[:, wide:].reshape(out_x.shape[1:])

    @pl.loop(0, spaces - 1)
    def _(i):
        to = away(i)
        for to_core in range(2):
            send(out_x.at[to_core, to], in_x.at[2 * i + core], 1, to_core, to)

    send(out_x.at[1 - core, space], in_x.at[peers - 2], 1, 1 - core, space)

    swap_rest.start()

    landed(in_own, recv_sems.at[0])
    mine = acc[span(space, 16), :]
    diag_ref[core, space] = mine + jnp.sum(in_own[...].astype(jnp.float32), axis=0)

    @pl.loop(0, spaces - 1)
    def _(i):
        send(diag_ref.at[core, space], diag_ref.at[core, space], 2, core, away(i))

    landed(in_x, recv_sems.at[1])
    mine = out_x[core, space].astype(jnp.float32)
    total = mine + jnp.sum(in_x[...].astype(jnp.float32), axis=0)
    cross_ref[me] = total.astype(cross_ref.dtype)

    @pl.loop(0, spaces - 1)
    def _(i):
        to = away(i)
        for to_core in range(2):
            send(cross_ref.at[me], cross_ref.at[me], 3, to_core, to)

    send(cross_ref.at[me], cross_ref.at[me], 3, 1 - core, space)

    landed(diag_ref.at[0, pl.ds(0, spaces - 1)], recv_sems.at[2])
    send(diag_ref.at[core], diag_ref.at[core], 4, 1 - core, space)
    landed(cross_ref.at[pl.ds(0, peers - 1)], recv_sems.at[3])
    landed(in_own, send_sems.at[0])
    landed(in_x, send_sems.at[1])
    landed(diag_ref.at[0, pl.ds(0, spaces - 1)], send_sems.at[2])
    landed(cross_ref.at[pl.ds(0, peers - 1)], send_sems.at[3])

    @pl.loop(0, chunks)
    def _(i):
        swap(i).wait_send()

    swap_rest.wait()
    for sems in (recv_sems, send_sems):
        landed(diag_ref.at[0], sems.at[4])


def subspace_kernel(points, diag_ref, cross_ref, sketch_ref, q_ref, corr_ref, high, low):
    k = corr_ref.shape[0]
    cross = cross_ref[...].astype(jnp.float32).reshape(k // 16, 2, 16, k // 2)
    corner = jnp.concatenate([cross[:, c].reshape(k, k // 2) for c in range(2)], axis=1)
    corner = corner.astype(jnp.bfloat16)
    high[:k, k:] = corner
    high[k:, :k] = corner.T
    for at in range(2):
        own = slice(at * k, at * k + k)
        whole = diag_ref[at].reshape(k, k)
        upper = whole.astype(jnp.bfloat16)
        high[own, own] = upper
        low[at] = (whole - upper.astype(jnp.float32)).astype(jnp.bfloat16)

    def times_gram(block):
        upper = block.astype(jnp.bfloat16)
        lower = (block - upper.astype(jnp.float32)).astype(jnp.bfloat16)
        small = [dot(upper[:, at * k : at * k + k], low[at], 1, 0, None) for at in range(2)]
        rest = dot(lower, high[...], 1, 0, None) + jnp.concatenate(small, axis=1)
        return dot(upper, high[...], 1, 0, None) + rest

    block = sketch_ref[...].T
    for _ in range(ITERS):
        y = times_gram(block)
        block = dot(inverse_factor(dot(y, y, 1, 1)), y, 1, 0)
    q_b = block.T.astype(jnp.bfloat16)
    q_ref[...] = q_b
    at = lax.rem(lax.axis_index("leaf"), 2)
    own = pl.ds(pl.multiple_of(at * k, k), k)
    term = dot(high[own, :], q_b, 1, 0, None) + dot(low[at], q_ref[own, :], 1, 0, None)
    corr_ref[...] = term * (1.0 / points)


def fresh_kernel(
    own_a, own_b, other_a, other_b, q_ref, corr_in, fresh_ref, corr_ref, held, sem, corr_sem
):
    corr_copy = pltpu.make_async_copy(corr_in, corr_ref.at[0], corr_sem)
    corr_copy.start()
    core = lax.rem(lax.axis_index("leaf"), 2)
    half, k = own_a.shape
    own = pl.ds(pl.multiple_of(core * k, k), k)
    rest = pl.ds(pl.multiple_of((1 - core) * k, k), k)
    weights = jnp.concatenate([q_ref[own, :], q_ref[rest, :]], axis=0)
    copies = []
    for part, (mine, other) in enumerate(((own_a, other_b), (own_b, other_a))):
        start = (1 - core if part == 0 else core) * half
        for i in range(half // TILE):
            rows = pl.ds(i * TILE, TILE)
            at = pl.ds(part * half + i * TILE, TILE)
            merged = jnp.concatenate([mine[rows, :], other[rows, :]], axis=1)
            held[at, :] = dot(merged, weights, 1, 0, None).astype(jnp.bfloat16)
            to = fresh_ref.at[0, pl.ds(pl.multiple_of(start + i * TILE, TILE), TILE)]
            copies.append(pltpu.make_async_copy(held.at[at], to, sem.at[len(copies)]))
            copies[-1].start()
    for copy in copies:
        copy.wait()
    corr_copy.wait()


def on_device(basis, sing_vals, sketch):
    rows, k = basis.shape[1:]
    spaces = lax.axis_size("space")
    points = rows * spaces
    half = rows // 2
    vmem = pl.BlockSpec(memory_space=pltpu.VMEM)
    any_space = pl.BlockSpec(memory_space=pl.ANY)
    f32, wire = jnp.float32, jnp.bfloat16
    chunks = half // CHUNK
    own_a, own_b, other_a, other_b, diag, cross = pl.pallas_call(
        exchange_kernel,
        out_shape=(
            pltpu.VMEM((half, k), jnp.bfloat16),
            pltpu.VMEM((half, k), jnp.bfloat16),
            pltpu.VMEM((half, k), jnp.bfloat16),
            pltpu.VMEM((half, k), jnp.bfloat16),
            pltpu.VMEM((2, spaces, k // spaces, k), f32),
            pltpu.VMEM((2 * spaces, k // spaces, k // 2), wire),
        ),
        in_specs=[pl.BlockSpec(memory_space=pltpu.HBM), vmem],
        out_specs=(vmem,) * 6,
        scratch_shapes=[
            pltpu.VMEM((chunks, k, CHUNK), jnp.bfloat16),
            pltpu.VMEM((k, k), f32),
            pltpu.VMEM((k, k), f32),
            pltpu.VMEM((spaces, k // spaces, k), wire),
            pltpu.VMEM((spaces - 1, k // spaces, k), wire),
            pltpu.VMEM((2, spaces, k // spaces, k // 2), wire),
            pltpu.VMEM((2 * spaces - 1, k // spaces, k // 2), wire),
            pltpu.SemaphoreType.REGULAR,
            pltpu.SemaphoreType.REGULAR,
            pltpu.SemaphoreType.DMA((chunks + half // STRIP,)),
            pltpu.SemaphoreType.DMA((chunks,)),
            pltpu.SemaphoreType.DMA((chunks,)),
            pltpu.SemaphoreType.DMA((2,)),
            pltpu.SemaphoreType.DMA((5,)),
            pltpu.SemaphoreType.DMA((5,)),
        ],
        compiler_params=pltpu.CompilerParams(
            collective_id=0, has_side_effects=True, vmem_limit_bytes=36 * 2**20
        ),
        name="exchange",
    )(basis, sing_vals)
    block_b, correlation = pl.pallas_call(
        functools.partial(subspace_kernel, points),
        out_shape=(
            jax.ShapeDtypeStruct(sketch.shape, jnp.bfloat16),
            pltpu.VMEM((k, k), f32),
        ),
        in_specs=[vmem, vmem, vmem],
        out_specs=(vmem, vmem),
        scratch_shapes=[
            pltpu.VMEM((2 * k, 2 * k), jnp.bfloat16),
            pltpu.VMEM((2, k, k), jnp.bfloat16),
        ],
        compiler_params=pltpu.CompilerParams(vmem_limit_bytes=16 * 2**20),
        cost_estimate=pl.CostEstimate(flops=2**31, bytes_accessed=80 * 2**20, transcendentals=0),
        name="subspace",
    )(diag, cross, sketch)
    return pl.pallas_call(
        fresh_kernel,
        out_shape=(
            jax.ShapeDtypeStruct((1, rows, k), jnp.bfloat16),
            jax.ShapeDtypeStruct((1, k, k), f32),
        ),
        in_specs=[vmem] * 6,
        out_specs=(any_space, any_space),
        scratch_shapes=[
            pltpu.VMEM((rows, k), jnp.bfloat16),
            pltpu.SemaphoreType.DMA((rows // TILE,)),
            pltpu.SemaphoreType.DMA,
        ],
        compiler_params=pltpu.CompilerParams(vmem_limit_bytes=32 * 2**20),
        name="fresh",
    )(own_a, own_b, other_a, other_b, block_b, correlation)


def solution(mesh):
    in_specs = (P("leaf", "space", None), P("leaf", None), P())
    out_specs = (P("leaf", "space", None), P("leaf", None, None))
    return jax.shard_map(
        on_device, mesh=mesh, in_specs=in_specs, out_specs=out_specs, check_vma=False
    )
```

```python
import functools
import jax
import jax.numpy as jnp
from jax import lax
from jax.experimental import pallas as pl
from jax.experimental.pallas import tpu as pltpu
from jax.sharding import PartitionSpec as P

ITERS = 2
PANEL = 32
SUB = 16
CHUNK = 2048
STRIP = 4096
TILE = 512
MESH = pl.DeviceIdType.MESH
EXACT = lax.Precision.HIGH


def dot(a, b, on_a, on_b, precision=EXACT):
    dims = (((on_a,), (on_b,)), ((), ()))
    return lax.dot_general(a, b, dims, precision=precision, preferred_element_type=jnp.float32)


def stack(block):
    terms = []
    for _ in range(3):
        terms.append(block.astype(jnp.bfloat16))
        block = block - terms[-1].astype(jnp.float32)
    high, mid, low = terms
    left = jnp.concatenate([high, mid, high, mid, low, high], axis=0)
    return left, jnp.concatenate([high, high, mid, mid, high, low], axis=0)


def inverse_factor(inner):
    n = inner.shape[0]
    count = n // PANEL
    tile = (8, 128)
    tall, wide = PANEL // 8, n // 128
    lane = lax.broadcasted_iota(jnp.int32, tile, 1)
    row = lax.broadcasted_iota(jnp.int32, tile, 0)
    lane_wide = lax.broadcasted_iota(jnp.int32, (PANEL, n), 1)
    unit = [jnp.where(row == s, 1.0, 0.0) for s in range(8)]
    shrink, grow = [], []
    for h in range(wide):
        corner = inner[128 * h : 128 * h + 128, 128 * h : 128 * h + 128]
        square = [lax.broadcasted_iota(jnp.int32, (128, 128), axis) for axis in range(2)]
        spots = jnp.sum(jnp.where(square[0] == square[1], corner, 0.0), axis=0, keepdims=True)
        spots = jnp.broadcast_to(spots, tile)
        shrink.append(lax.rsqrt(spots))
        grow.append(spots * shrink[h])
    panels = [inner[i * PANEL : (i + 1) * PANEL] for i in range(count)]
    done = []
    for p in range(count):
        first = p * PANEL
        here, base = first // 128, first % 128
        w = [
            [panels[p][8 * r : 8 * r + 8, 128 * h : 128 * h + 128] for h in range(wide)]
            for r in range(tall)
        ]
        diag = [jnp.zeros(tile, jnp.float32)] * tall
        for sub in range(0, PANEL, SUB):
            near_cols = {r: w[r][here] * shrink[here] for r in range(sub // 8, tall)}
            spots = [base + sub + j for j in range(SUB)]
            cols = [
                {r: jnp.broadcast_to(value[:, at : at + 1], tile) for r, value in near_cols.items()}
                for at in spots
            ]
            back = [jnp.broadcast_to(grow[here][:, at : at + 1], tile) for at in spots]
            for j in range(0, SUB, 2):
                at = sub + j
                top, s = at // 8, at % 8
                one, two = cols[j], cols[j + 1]
                a, b = (jnp.broadcast_to(one[top][s + t : s + t + 1], tile) for t in range(2))
                c, d = (jnp.broadcast_to(two[top][s + t : s + t + 1], tile) for t in range(2))
                det = a * d - b * c
                inv_det, inv_a = 1.0 / det, 1.0 / a
                left = {r: (d * one[r] - b * two[r]) * inv_det for r in range(top, tall)}
                right = {r: (a * two[r] - c * one[r]) * inv_det for r in range(top, tall)}
                left[top] = jnp.where(row > s + 1, left[top], 0.0)
                right[top] = jnp.where(row > s + 1, right[top], 0.0)
                if s == 6:
                    del left[top], right[top]
                for k in range(j + 2, SUB):
                    e, f = cols[k][top][s : s + 1], cols[k][top][s + 1 : s + 2]
                    for r in left:
                        cols[k][r] = (cols[k][r] - left[r] * e) - right[r] * f
                diag[top] = jnp.where(row == s, a * back[j], diag[top])
                diag[top] = jnp.where(row == s + 1, det * inv_a * back[j + 1], diag[top])
                for t in range(2):
                    at_lane = lane == base + at + t
                    w[top][here] = jnp.where(at_lane, unit[s + t], w[top][here])
                    for r in range(top + 1, tall):
                        w[r][here] = jnp.where(at_lane, 0.0, w[r][here])
                low = jnp.where(row == s + 1, b * inv_a, 0.0)
                for h in range(wide):
                    e, f = w[top][h][s : s + 1], w[top][h][s + 1 : s + 2]
                    for r in left:
                        w[r][h] = (w[r][h] - left[r] * e) - right[r] * f
                    w[top][h] = w[top][h] - low * e
        for r in range(tall):
            scale = lax.rsqrt(diag[r])
            w[r] = [value * scale for value in w[r]]
            if r + 1 < tall:
                above = (lane >= base + 8 * r + 8) & (lane < base + PANEL)
                w[r][here] = jnp.where(above, 0.0, w[r][here])
        block = jnp.concatenate([jnp.concatenate(tiles, axis=1) for tiles in w], axis=0)
        after = first + PANEL
        if after == n:
            done.append(block)
            break
        done.append(jnp.where(lane_wide < after, block, 0.0))
        blank = (lane_wide >= first) & (lane_wide < after)
        stacked, terms = stack(block)
        turned = [stacked[:, 128 * h : 128 * h + 128].T for h in range(wide)]
        near = dot(turned[after // 128][after % 128 : after % 128 + PANEL], terms, 1, 0, None)
        panels[p + 1] = jnp.where(blank, 0.0, panels[p + 1]) - near
        if after + PANEL < n:
            far = dot(jnp.concatenate(turned, axis=0)[after + PANEL :], terms, 1, 0, None)
            for m in range(p + 2, count):
                at = (m - p - 2) * PANEL
                panels[m] = jnp.where(blank, 0.0, panels[m]) - far[at : at + PANEL]
    return jnp.concatenate(done, axis=0)


def exchange_kernel(
    basis_ref, sing_ref, own_a, own_b, other_a, other_b, diag_ref, cross_ref,
    turned, acc, acc_x, out_own, in_own, out_x, in_x,
    answer, entered, load_sem, swap_send, swap_recv, rest_sems, send_sems, recv_sems,
):
    leaf, space = lax.axis_index("leaf"), lax.axis_index("space")
    spaces = lax.axis_size("space")
    peers = 2 * spaces
    core, pair = lax.rem(leaf, 2), lax.div(leaf, 2)
    me = space * 2 + core
    partner = (leaf + 1 - 2 * core, space)
    half = own_a.shape[0]
    chunks, strips = half // CHUNK, half // STRIP

    def away(i):
        side = 4
        k, m = lax.div(i, side), lax.rem(i, side)
        dy = lax.rem(2 + k + lax.div(k, 2) * (5 - 2 * k), side)
        dz = lax.rem(2 + m + lax.div(m, 2) * (5 - 2 * m), side)
        y, z = lax.div(space, side), lax.rem(space, side)
        return lax.rem(y + dy, side) * side + lax.rem(z + dz, side)

    def span(i, size, start=0):
        return pl.ds(pl.multiple_of(start + i * size, size), size)

    def load(part, start, i, size, sem):
        return pltpu.make_async_copy(
            basis_ref.at[0, span(i, size, start)], part.at[span(i, size)], sem
        )

    def scale(part, i, size):
        rows = span(i, size)
        part[rows, :] = (part[rows, :].astype(jnp.float32) * sing_ref[...]).astype(jnp.bfloat16)

    def swap(i):
        return pltpu.make_async_remote_copy(
            src_ref=own_a.at[span(i, CHUNK)], dst_ref=other_a.at[span(i, CHUNK)],
            send_sem=swap_send.at[i], recv_sem=swap_recv.at[i],
            device_id=partner, device_id_type=MESH,
        )

    swap_rest = pltpu.make_async_remote_copy(
        src_ref=own_b, dst_ref=other_b, send_sem=rest_sems.at[0], recv_sem=rest_sems.at[1],
        device_id=partner, device_id_type=MESH,
    )

    def send(src, dst, which, to_core, to_space):
        pltpu.make_async_remote_copy(
            src_ref=src, dst_ref=dst, send_sem=send_sems.at[which], recv_sem=recv_sems.at[which],
            device_id=(pair * 2 + to_core, to_space), device_id_type=MESH,
        ).start()

    def landed(ref, sem):
        pltpu.make_async_copy(ref, ref, sem).wait()

    first, second = (1 - core) * half, core * half
    for i in range(chunks):
        load(own_a, first, i, CHUNK, load_sem.at[i]).start()
    for i in range(strips):
        load(own_b, second, i, STRIP, load_sem.at[chunks + i]).start()

    barrier = pltpu.get_barrier_semaphore()

    @pl.when(core == 1)
    def _():
        pl.semaphore_signal(barrier, inc=1, device_id=partner, device_id_type=MESH)

    @pl.when(core == 0)
    def _():
        pl.semaphore_wait(barrier, 1)
        pl.semaphore_signal(answer, inc=1, device_id=partner, device_id_type=MESH)

    @pl.when(core == 1)
    def _():
        pl.semaphore_wait(answer, 1)

        @pl.loop(0, spaces - 1)
        def _(i):
            pl.semaphore_signal(
                barrier, inc=1, device_id=(leaf, away(i)), device_id_type=MESH
            )

    acc[...] = jnp.zeros_like(acc)
    acc_x[...] = jnp.zeros_like(acc_x)
    load(own_a, first, 0, CHUNK, load_sem.at[0]).wait()
    scale(own_a, 0, CHUNK)
    swap(0).start()

    @pl.loop(1, chunks)
    def _(i):
        load(own_a, first, i, CHUNK, load_sem.at[i]).wait()
        scale(own_a, i, CHUNK)
        swap(i).start()

    @pl.loop(0, strips)
    def _(i):
        value = own_a[span(i, STRIP), :]
        acc[...] += dot(value, value, 0, 0, None)

    @pl.loop(0, strips)
    def _(i):
        load(own_b, second, i, STRIP, load_sem.at[chunks + i]).wait()
        scale(own_b, i, STRIP)
        value = own_b[span(i, STRIP), :]
        flipped = value.T
        for part in range(STRIP // CHUNK):
            turned[i * (STRIP // CHUNK) + part] = flipped[:, part * CHUNK : (part + 1) * CHUNK]
        acc[...] += dot(flipped, value, 1, 0, None)

    @pl.when(core == 1)
    def _():
        pl.semaphore_wait(barrier, spaces - 1)
        pl.semaphore_signal(entered, inc=1, device_id=partner, device_id_type=MESH)

    @pl.when(core == 0)
    def _():
        pl.semaphore_wait(entered, 1)

    out_own[...] = acc[...].astype(out_own.dtype).reshape(out_own.shape)

    @pl.loop(0, spaces - 1)
    def _(i):
        to = away(i)
        send(out_own.at[to], in_own.at[i], 0, core, to)

    def add_cross(i):
        swap(i).wait_recv()
        acc_x[...] += dot(turned[i], other_a[span(i, CHUNK), :], 1, 0, None)

    @pl.loop(0, chunks)
    def _(i):
        add_cross(i)

    cross = acc_x[...].astype(out_x.dtype)
    cross = jnp.where(core == 0, cross, cross.T)
    wide = cross.shape[1] // 2
    out_x[0] = cross[:, :wide].reshape(out_x.shape[1:])
    out_x[1] = cross[:, wide:].reshape(out_x.shape[1:])

    @pl.loop(0, spaces - 1)
    def _(i):
        to = away(i)
        for to_core in range(2):
            send(out_x.at[to_core, to], in_x.at[2 * i + core], 1, to_core, to)

    send(out_x.at[1 - core, space], in_x.at[peers - 2], 1, 1 - core, space)

    swap_rest.start()

    landed(in_own, recv_sems.at[0])
    mine = acc[span(space, 16), :]
    diag_ref[core, space] = mine + jnp.sum(in_own[...].astype(jnp.float32), axis=0)

    @pl.loop(0, spaces - 1)
    def _(i):
        send(diag_ref.at[core, space], diag_ref.at[core, space], 2, core, away(i))

    landed(in_x, recv_sems.at[1])
    mine = out_x[core, space].astype(jnp.float32)
    total = mine + jnp.sum(in_x[...].astype(jnp.float32), axis=0)
    cross_ref[me] = total.astype(cross_ref.dtype)

    @pl.loop(0, spaces - 1)
    def _(i):
        to = away(i)
        for to_core in range(2):
            send(cross_ref.at[me], cross_ref.at[me], 3, to_core, to)

    send(cross_ref.at[me], cross_ref.at[me], 3, 1 - core, space)

    landed(diag_ref.at[0, pl.ds(0, spaces - 1)], recv_sems.at[2])
    send(diag_ref.at[core], diag_ref.at[core], 4, 1 - core, space)
    landed(cross_ref.at[pl.ds(0, peers - 1)], recv_sems.at[3])
    landed(in_own, send_sems.at[0])
    landed(in_x, send_sems.at[1])
    landed(diag_ref.at[0, pl.ds(0, spaces - 1)], send_sems.at[2])
    landed(cross_ref.at[pl.ds(0, peers - 1)], send_sems.at[3])

    @pl.loop(0, chunks)
    def _(i):
        swap(i).wait_send()

    swap_rest.wait()
    for sems in (recv_sems, send_sems):
        landed(diag_ref.at[0], sems.at[4])


def finish_kernel(
    points, diag_ref, cross_ref, sketch_ref, own_a, own_b, other_a, other_b, fresh_ref, corr_ref,
    high, low, q_ref, corr, held, sem, corr_sem,
):
    half, k = own_a.shape
    cross = cross_ref[...].astype(jnp.float32).reshape(k // 16, 2, 16, k // 2)
    corner = jnp.concatenate([cross[:, c].reshape(k, k // 2) for c in range(2)], axis=1)
    corner = corner.astype(jnp.bfloat16)
    high[:k, k:] = corner
    high[k:, :k] = corner.T
    for at in range(2):
        own = slice(at * k, at * k + k)
        whole = diag_ref[at].reshape(k, k)
        upper = whole.astype(jnp.bfloat16)
        high[own, own] = upper
        low[at] = (whole - upper.astype(jnp.float32)).astype(jnp.bfloat16)

    def times_gram(block):
        upper = block.astype(jnp.bfloat16)
        lower = (block - upper.astype(jnp.float32)).astype(jnp.bfloat16)
        small = [dot(upper[:, at * k : at * k + k], low[at], 1, 0, None) for at in range(2)]
        rest = dot(lower, high[...], 1, 0, None) + jnp.concatenate(small, axis=1)
        return dot(upper, high[...], 1, 0, None) + rest

    block = sketch_ref[...].T
    for _ in range(ITERS):
        y = times_gram(block)
        block = dot(inverse_factor(dot(y, y, 1, 1)), y, 1, 0)
    q_b = block.T.astype(jnp.bfloat16)
    q_ref[...] = q_b
    core = lax.rem(lax.axis_index("leaf"), 2)
    own = pl.ds(pl.multiple_of(core * k, k), k)
    rest = pl.ds(pl.multiple_of((1 - core) * k, k), k)
    weights = jnp.concatenate([q_ref[own, :], q_ref[rest, :]], axis=0)
    copies = []
    for part, (mine, other) in enumerate(((own_a, other_b), (own_b, other_a))):
        start = (1 - core if part == 0 else core) * half
        for i in range(half // TILE):
            rows = pl.ds(i * TILE, TILE)
            at = pl.ds(part * half + i * TILE, TILE)
            merged = jnp.concatenate([mine[rows, :], other[rows, :]], axis=1)
            held[at, :] = dot(merged, weights, 1, 0, None).astype(jnp.bfloat16)
            to = fresh_ref.at[0, pl.ds(pl.multiple_of(start + i * TILE, TILE), TILE)]
            copies.append(pltpu.make_async_copy(held.at[at], to, sem.at[part * (half // TILE) + i]))
            copies[-1].start()
        if part == 0:
            term = dot(high[own, :], q_b, 1, 0, None) + dot(low[core], q_ref[own, :], 1, 0, None)
            corr[...] = term * (1.0 / points)
            copies.append(pltpu.make_async_copy(corr, corr_ref.at[0], corr_sem))
            copies[-1].start()
    for copy in copies:
        copy.wait()


def on_device(basis, sing_vals, sketch):
    rows, k = basis.shape[1:]
    spaces = lax.axis_size("space")
    points = rows * spaces
    half = rows // 2
    vmem = pl.BlockSpec(memory_space=pltpu.VMEM)
    any_space = pl.BlockSpec(memory_space=pl.ANY)
    f32, wire = jnp.float32, jnp.bfloat16
    chunks = half // CHUNK
    own_a, own_b, other_a, other_b, diag, cross = pl.pallas_call(
        exchange_kernel,
        out_shape=(
            pltpu.VMEM((half, k), jnp.bfloat16),
            pltpu.VMEM((half, k), jnp.bfloat16),
            pltpu.VMEM((half, k), jnp.bfloat16),
            pltpu.VMEM((half, k), jnp.bfloat16),
            pltpu.VMEM((2, spaces, k // spaces, k), f32),
            pltpu.VMEM((2 * spaces, k // spaces, k // 2), wire),
        ),
        in_specs=[pl.BlockSpec(memory_space=pltpu.HBM), vmem],
        out_specs=(vmem,) * 6,
        scratch_shapes=[
            pltpu.VMEM((chunks, k, CHUNK), jnp.bfloat16),
            pltpu.VMEM((k, k), f32),
            pltpu.VMEM((k, k), f32),
            pltpu.VMEM((spaces, k // spaces, k), wire),
            pltpu.VMEM((spaces - 1, k // spaces, k), wire),
            pltpu.VMEM((2, spaces, k // spaces, k // 2), wire),
            pltpu.VMEM((2 * spaces - 1, k // spaces, k // 2), wire),
            pltpu.SemaphoreType.REGULAR,
            pltpu.SemaphoreType.REGULAR,
            pltpu.SemaphoreType.DMA((chunks + half // STRIP,)),
            pltpu.SemaphoreType.DMA((chunks,)),
            pltpu.SemaphoreType.DMA((chunks,)),
            pltpu.SemaphoreType.DMA((2,)),
            pltpu.SemaphoreType.DMA((5,)),
            pltpu.SemaphoreType.DMA((5,)),
        ],
        compiler_params=pltpu.CompilerParams(
            collective_id=0, has_side_effects=True, vmem_limit_bytes=36 * 2**20
        ),
        name="exchange",
    )(basis, sing_vals)
    return pl.pallas_call(
        functools.partial(finish_kernel, points),
        out_shape=(
            jax.ShapeDtypeStruct((1, rows, k), jnp.bfloat16),
            jax.ShapeDtypeStruct((1, k, k), f32),
        ),
        in_specs=[vmem] * 7,
        out_specs=(any_space, any_space),
        scratch_shapes=[
            pltpu.VMEM((2 * k, 2 * k), jnp.bfloat16),
            pltpu.VMEM((2, k, k), jnp.bfloat16),
            pltpu.VMEM((2 * k, k), jnp.bfloat16),
            pltpu.VMEM((k, k), f32),
            pltpu.VMEM((rows, k), jnp.bfloat16),
            pltpu.SemaphoreType.DMA((rows // TILE,)),
            pltpu.SemaphoreType.DMA,
        ],
        compiler_params=pltpu.CompilerParams(vmem_limit_bytes=36 * 2**20),
        name="finish",
    )(diag, cross, sketch, own_a, own_b, other_a, other_b)


def solution(mesh):
    in_specs = (P("leaf", "space", None), P("leaf", None), P())
    out_specs = (P("leaf", "space", None), P("leaf", None, None))
    return jax.shard_map(
        on_device, mesh=mesh, in_specs=in_specs, out_specs=out_specs, check_vma=False
    )
```

```python
import functools
import jax
import jax.numpy as jnp
from jax import lax
from jax.experimental import pallas as pl
from jax.experimental.pallas import tpu as pltpu
from jax.sharding import PartitionSpec as P

ITERS = 2
PANEL = 32
SUB = 16
CHUNK = 2048
STRIP = 4096
TILE = 512
MESH = pl.DeviceIdType.MESH
EXACT = lax.Precision.HIGH


def dot(a, b, on_a, on_b, precision=EXACT):
    dims = (((on_a,), (on_b,)), ((), ()))
    return lax.dot_general(a, b, dims, precision=precision, preferred_element_type=jnp.float32)


def stack(block):
    terms = []
    for _ in range(3):
        terms.append(block.astype(jnp.bfloat16))
        block = block - terms[-1].astype(jnp.float32)
    high, mid, low = terms
    left = jnp.concatenate([high, mid, high, mid, low, high], axis=0)
    return left, jnp.concatenate([high, high, mid, mid, high, low], axis=0)


def inverse_factor(inner):
    n = inner.shape[0]
    count = n // PANEL
    tile = (8, 128)
    tall, wide = PANEL // 8, n // 128
    lane = lax.broadcasted_iota(jnp.int32, tile, 1)
    row = lax.broadcasted_iota(jnp.int32, tile, 0)
    lane_wide = lax.broadcasted_iota(jnp.int32, (PANEL, n), 1)
    unit = [jnp.where(row == s, 1.0, 0.0) for s in range(8)]
    shrink, grow = [], []
    for h in range(wide):
        corner = inner[128 * h : 128 * h + 128, 128 * h : 128 * h + 128]
        square = [lax.broadcasted_iota(jnp.int32, (128, 128), axis) for axis in range(2)]
        spots = jnp.sum(jnp.where(square[0] == square[1], corner, 0.0), axis=0, keepdims=True)
        spots = jnp.broadcast_to(spots, tile)
        shrink.append(lax.rsqrt(spots))
        grow.append(spots * shrink[h])
    panels = [inner[i * PANEL : (i + 1) * PANEL] for i in range(count)]
    done = []
    for p in range(count):
        first = p * PANEL
        here, base = first // 128, first % 128
        w = [
            [panels[p][8 * r : 8 * r + 8, 128 * h : 128 * h + 128] for h in range(wide)]
            for r in range(tall)
        ]
        diag = [jnp.zeros(tile, jnp.float32)] * tall
        for sub in range(0, PANEL, SUB):
            near_cols = {r: w[r][here] * shrink[here] for r in range(sub // 8, tall)}
            spots = [base + sub + j for j in range(SUB)]
            cols = [
                {r: jnp.broadcast_to(value[:, at : at + 1], tile) for r, value in near_cols.items()}
                for at in spots
            ]
            back = [jnp.broadcast_to(grow[here][:, at : at + 1], tile) for at in spots]
            for j in range(0, SUB, 2):
                at = sub + j
                top, s = at // 8, at % 8
                one, two = cols[j], cols[j + 1]
                a, b = (jnp.broadcast_to(one[top][s + t : s + t + 1], tile) for t in range(2))
                c, d = (jnp.broadcast_to(two[top][s + t : s + t + 1], tile) for t in range(2))
                det = a * d - b * c
                inv_det, inv_a = 1.0 / det, 1.0 / a
                left = {r: (d * one[r] - b * two[r]) * inv_det for r in range(top, tall)}
                right = {r: (a * two[r] - c * one[r]) * inv_det for r in range(top, tall)}
                left[top] = jnp.where(row > s + 1, left[top], 0.0)
                right[top] = jnp.where(row > s + 1, right[top], 0.0)
                if s == 6:
                    del left[top], right[top]
                for k in range(j + 2, SUB):
                    e, f = cols[k][top][s : s + 1], cols[k][top][s + 1 : s + 2]
                    for r in left:
                        cols[k][r] = (cols[k][r] - left[r] * e) - right[r] * f
                diag[top] = jnp.where(row == s, a * back[j], diag[top])
                diag[top] = jnp.where(row == s + 1, det * inv_a * back[j + 1], diag[top])
                for t in range(2):
                    at_lane = lane == base + at + t
                    w[top][here] = jnp.where(at_lane, unit[s + t], w[top][here])
                    for r in range(top + 1, tall):
                        w[r][here] = jnp.where(at_lane, 0.0, w[r][here])
                low = jnp.where(row == s + 1, b * inv_a, 0.0)
                for h in range(wide):
                    e, f = w[top][h][s : s + 1], w[top][h][s + 1 : s + 2]
                    for r in left:
                        w[r][h] = (w[r][h] - left[r] * e) - right[r] * f
                    w[top][h] = w[top][h] - low * e
        for r in range(tall):
            scale = lax.rsqrt(diag[r])
            w[r] = [value * scale for value in w[r]]
            if r + 1 < tall:
                above = (lane >= base + 8 * r + 8) & (lane < base + PANEL)
                w[r][here] = jnp.where(above, 0.0, w[r][here])
        block = jnp.concatenate([jnp.concatenate(tiles, axis=1) for tiles in w], axis=0)
        after = first + PANEL
        if after == n:
            done.append(block)
            break
        done.append(jnp.where(lane_wide < after, block, 0.0))
        blank = (lane_wide >= first) & (lane_wide < after)
        stacked, terms = stack(block)
        turned = [stacked[:, 128 * h : 128 * h + 128].T for h in range(wide)]
        near = dot(turned[after // 128][after % 128 : after % 128 + PANEL], terms, 1, 0, None)
        panels[p + 1] = jnp.where(blank, 0.0, panels[p + 1]) - near
        if after + PANEL < n:
            far = dot(jnp.concatenate(turned, axis=0)[after + PANEL :], terms, 1, 0, None)
            for m in range(p + 2, count):
                at = (m - p - 2) * PANEL
                panels[m] = jnp.where(blank, 0.0, panels[m]) - far[at : at + PANEL]
    return jnp.concatenate(done, axis=0)


def exchange_kernel(
    basis_ref, sing_ref, own_a, own_b, other_a, other_b, diag_ref, cross_ref,
    turned, acc, acc_x, out_own, in_own, out_x, in_x,
    answer, entered, load_sem, swap_send, swap_recv, rest_sems, send_sems, recv_sems,
):
    leaf, space = lax.axis_index("leaf"), lax.axis_index("space")
    spaces = lax.axis_size("space")
    peers = 2 * spaces
    core, pair = lax.rem(leaf, 2), lax.div(leaf, 2)
    me = space * 2 + core
    partner = (leaf + 1 - 2 * core, space)
    half = own_a.shape[0]
    chunks, strips = half // CHUNK, half // STRIP

    def away(i):
        side = 4
        k, m = lax.div(i, side), lax.rem(i, side)
        dy = lax.rem(2 + k + lax.div(k, 2) * (5 - 2 * k), side)
        dz = lax.rem(2 + m + lax.div(m, 2) * (5 - 2 * m), side)
        y, z = lax.div(space, side), lax.rem(space, side)
        return lax.rem(y + dy, side) * side + lax.rem(z + dz, side)

    def span(i, size, start=0):
        return pl.ds(pl.multiple_of(start + i * size, size), size)

    def load(part, start, i, size, sem):
        return pltpu.make_async_copy(
            basis_ref.at[0, span(i, size, start)], part.at[span(i, size)], sem
        )

    def scale(part, i, size):
        rows = span(i, size)
        part[rows, :] = (part[rows, :].astype(jnp.float32) * sing_ref[...]).astype(jnp.bfloat16)

    def swap(i):
        return pltpu.make_async_remote_copy(
            src_ref=own_a.at[span(i, CHUNK)], dst_ref=other_a.at[span(i, CHUNK)],
            send_sem=swap_send.at[i], recv_sem=swap_recv.at[i],
            device_id=partner, device_id_type=MESH,
        )

    swap_rest = pltpu.make_async_remote_copy(
        src_ref=own_b, dst_ref=other_b, send_sem=rest_sems.at[0], recv_sem=rest_sems.at[1],
        device_id=partner, device_id_type=MESH,
    )

    def send(src, dst, which, to_core, to_space):
        pltpu.make_async_remote_copy(
            src_ref=src, dst_ref=dst, send_sem=send_sems.at[which], recv_sem=recv_sems.at[which],
            device_id=(pair * 2 + to_core, to_space), device_id_type=MESH,
        ).start()

    def landed(ref, sem):
        pltpu.make_async_copy(ref, ref, sem).wait()

    first, second = (1 - core) * half, core * half
    for i in range(chunks):
        load(own_a, first, i, CHUNK, load_sem.at[i]).start()
    for i in range(strips):
        load(own_b, second, i, STRIP, load_sem.at[chunks + i]).start()

    barrier = pltpu.get_barrier_semaphore()

    @pl.when(core == 1)
    def _():
        pl.semaphore_signal(barrier, inc=1, device_id=partner, device_id_type=MESH)

    @pl.when(core == 0)
    def _():
        pl.semaphore_wait(barrier, 1)
        pl.semaphore_signal(answer, inc=1, device_id=partner, device_id_type=MESH)

    @pl.when(core == 1)
    def _():
        pl.semaphore_wait(answer, 1)

        @pl.loop(0, spaces - 1)
        def _(i):
            pl.semaphore_signal(
                barrier, inc=1, device_id=(leaf, away(i)), device_id_type=MESH
            )

    acc[...] = jnp.zeros_like(acc)
    acc_x[...] = jnp.zeros_like(acc_x)
    load(own_a, first, 0, CHUNK, load_sem.at[0]).wait()
    scale(own_a, 0, CHUNK)
    swap(0).start()

    @pl.loop(1, chunks)
    def _(i):
        load(own_a, first, i, CHUNK, load_sem.at[i]).wait()
        scale(own_a, i, CHUNK)
        swap(i).start()

    @pl.loop(0, strips)
    def _(i):
        value = own_a[span(i, STRIP), :]
        acc[...] += dot(value, value, 0, 0, None)

    @pl.loop(0, strips)
    def _(i):
        load(own_b, second, i, STRIP, load_sem.at[chunks + i]).wait()
        scale(own_b, i, STRIP)
        value = own_b[span(i, STRIP), :]
        flipped = value.T
        for part in range(STRIP // CHUNK):
            turned[i * (STRIP // CHUNK) + part] = flipped[:, part * CHUNK : (part + 1) * CHUNK]
        acc[...] += dot(flipped, value, 1, 0, None)

    @pl.when(core == 1)
    def _():
        pl.semaphore_wait(barrier, spaces - 1)
        pl.semaphore_signal(entered, inc=1, device_id=partner, device_id_type=MESH)

    @pl.when(core == 0)
    def _():
        pl.semaphore_wait(entered, 1)

    out_own[...] = acc[...].astype(out_own.dtype).reshape(out_own.shape)

    @pl.loop(0, spaces - 1)
    def _(i):
        to = away(i)
        send(out_own.at[to], in_own.at[i], 0, core, to)

    def add_cross(i):
        swap(i).wait_recv()
        acc_x[...] += dot(turned[i], other_a[span(i, CHUNK), :], 1, 0, None)

    @pl.loop(0, chunks)
    def _(i):
        add_cross(i)

    cross = acc_x[...].astype(out_x.dtype)
    cross = jnp.where(core == 0, cross, cross.T)
    wide = cross.shape[1] // 2
    out_x[0] = cross[:, :wide].reshape(out_x.shape[1:])
    out_x[1] = cross[:, wide:].reshape(out_x.shape[1:])

    @pl.loop(0, spaces - 1)
    def _(i):
        to = away(i)
        for to_core in range(2):
            send(out_x.at[to_core, to], in_x.at[2 * i + core], 1, to_core, to)

    send(out_x.at[1 - core, space], in_x.at[peers - 2], 1, 1 - core, space)

    swap_rest.start()

    landed(in_own, recv_sems.at[0])
    mine = acc[span(space, 16), :]
    diag_ref[core, space] = mine + jnp.sum(in_own[...].astype(jnp.float32), axis=0)

    @pl.loop(0, spaces - 1)
    def _(i):
        send(diag_ref.at[core, space], diag_ref.at[core, space], 2, core, away(i))

    landed(in_x, recv_sems.at[1])
    mine = out_x[core, space].astype(jnp.float32)
    total = mine + jnp.sum(in_x[...].astype(jnp.float32), axis=0)
    cross_ref[me] = total.astype(cross_ref.dtype)

    @pl.loop(0, spaces - 1)
    def _(i):
        to = away(i)
        for to_core in range(2):
            send(cross_ref.at[me], cross_ref.at[me], 3, to_core, to)

    send(cross_ref.at[me], cross_ref.at[me], 3, 1 - core, space)

    landed(diag_ref.at[0, pl.ds(0, spaces - 1)], recv_sems.at[2])
    send(diag_ref.at[core], diag_ref.at[core], 4, 1 - core, space)
    landed(cross_ref.at[pl.ds(0, peers - 1)], recv_sems.at[3])
    landed(in_own, send_sems.at[0])
    landed(in_x, send_sems.at[1])
    landed(diag_ref.at[0, pl.ds(0, spaces - 1)], send_sems.at[2])
    landed(cross_ref.at[pl.ds(0, peers - 1)], send_sems.at[3])

    @pl.loop(0, chunks)
    def _(i):
        swap(i).wait_send()

    swap_rest.wait()
    for sems in (recv_sems, send_sems):
        landed(diag_ref.at[0], sems.at[4])


def finish_kernel(
    points, diag_ref, cross_ref, sketch_ref, own_a, own_b, other_a, other_b, fresh_ref, corr_ref,
    high, low, q_ref, corr, held, sem, corr_sem,
):
    half, k = own_a.shape
    cross = cross_ref[...].astype(jnp.float32).reshape(k // 16, 2, 16, k // 2)
    corner = jnp.concatenate([cross[:, c].reshape(k, k // 2) for c in range(2)], axis=1)
    corner = corner.astype(jnp.bfloat16)
    high[:k, k:] = corner
    high[k:, :k] = corner.T
    for at in range(2):
        own = slice(at * k, at * k + k)
        whole = diag_ref[at].reshape(k, k)
        upper = whole.astype(jnp.bfloat16)
        high[own, own] = upper
        low[at] = (whole - upper.astype(jnp.float32)).astype(jnp.bfloat16)

    def times_gram(block):
        upper = block.astype(jnp.bfloat16)
        lower = (block - upper.astype(jnp.float32)).astype(jnp.bfloat16)
        small = [dot(upper[:, at * k : at * k + k], low[at], 1, 0, None) for at in range(2)]
        rest = dot(lower, high[...], 1, 0, None) + jnp.concatenate(small, axis=1)
        return dot(upper, high[...], 1, 0, None) + rest

    y = times_gram(sketch_ref[...].T)
    for _ in range(ITERS - 1):
        ahead = times_gram(y)
        y = dot(inverse_factor(dot(y, y, 1, 1)), ahead, 1, 0)
    block = dot(inverse_factor(dot(y, y, 1, 1)), y, 1, 0)
    q_b = block.T.astype(jnp.bfloat16)
    q_ref[...] = q_b
    core = lax.rem(lax.axis_index("leaf"), 2)
    own = pl.ds(pl.multiple_of(core * k, k), k)
    rest = pl.ds(pl.multiple_of((1 - core) * k, k), k)
    weights = jnp.concatenate([q_ref[own, :], q_ref[rest, :]], axis=0)
    copies = []
    for part, (mine, other) in enumerate(((own_a, other_b), (own_b, other_a))):
        start = (1 - core if part == 0 else core) * half
        for i in range(half // TILE):
            rows = pl.ds(i * TILE, TILE)
            at = pl.ds(part * half + i * TILE, TILE)
            merged = jnp.concatenate([mine[rows, :], other[rows, :]], axis=1)
            held[at, :] = dot(merged, weights, 1, 0, None).astype(jnp.bfloat16)
            to = fresh_ref.at[0, pl.ds(pl.multiple_of(start + i * TILE, TILE), TILE)]
            copies.append(pltpu.make_async_copy(held.at[at], to, sem.at[part * (half // TILE) + i]))
            copies[-1].start()
        if part == 0:
            term = dot(high[own, :], q_b, 1, 0, None) + dot(low[core], q_ref[own, :], 1, 0, None)
            corr[...] = term * (1.0 / points)
            copies.append(pltpu.make_async_copy(corr, corr_ref.at[0], corr_sem))
            copies[-1].start()
    for copy in copies:
        copy.wait()


def on_device(basis, sing_vals, sketch):
    rows, k = basis.shape[1:]
    spaces = lax.axis_size("space")
    points = rows * spaces
    half = rows // 2
    vmem = pl.BlockSpec(memory_space=pltpu.VMEM)
    any_space = pl.BlockSpec(memory_space=pl.ANY)
    f32, wire = jnp.float32, jnp.bfloat16
    chunks = half // CHUNK
    own_a, own_b, other_a, other_b, diag, cross = pl.pallas_call(
        exchange_kernel,
        out_shape=(
            pltpu.VMEM((half, k), jnp.bfloat16),
            pltpu.VMEM((half, k), jnp.bfloat16),
            pltpu.VMEM((half, k), jnp.bfloat16),
            pltpu.VMEM((half, k), jnp.bfloat16),
            pltpu.VMEM((2, spaces, k // spaces, k), f32),
            pltpu.VMEM((2 * spaces, k // spaces, k // 2), wire),
        ),
        in_specs=[pl.BlockSpec(memory_space=pltpu.HBM), vmem],
        out_specs=(vmem,) * 6,
        scratch_shapes=[
            pltpu.VMEM((chunks, k, CHUNK), jnp.bfloat16),
            pltpu.VMEM((k, k), f32),
            pltpu.VMEM((k, k), f32),
            pltpu.VMEM((spaces, k // spaces, k), wire),
            pltpu.VMEM((spaces - 1, k // spaces, k), wire),
            pltpu.VMEM((2, spaces, k // spaces, k // 2), wire),
            pltpu.VMEM((2 * spaces - 1, k // spaces, k // 2), wire),
            pltpu.SemaphoreType.REGULAR,
            pltpu.SemaphoreType.REGULAR,
            pltpu.SemaphoreType.DMA((chunks + half // STRIP,)),
            pltpu.SemaphoreType.DMA((chunks,)),
            pltpu.SemaphoreType.DMA((chunks,)),
            pltpu.SemaphoreType.DMA((2,)),
            pltpu.SemaphoreType.DMA((5,)),
            pltpu.SemaphoreType.DMA((5,)),
        ],
        compiler_params=pltpu.CompilerParams(
            collective_id=0, has_side_effects=True, vmem_limit_bytes=36 * 2**20
        ),
        name="exchange",
    )(basis, sing_vals)
    return pl.pallas_call(
        functools.partial(finish_kernel, points),
        out_shape=(
            jax.ShapeDtypeStruct((1, rows, k), jnp.bfloat16),
            jax.ShapeDtypeStruct((1, k, k), f32),
        ),
        in_specs=[vmem] * 7,
        out_specs=(any_space, any_space),
        scratch_shapes=[
            pltpu.VMEM((2 * k, 2 * k), jnp.bfloat16),
            pltpu.VMEM((2, k, k), jnp.bfloat16),
            pltpu.VMEM((2 * k, k), jnp.bfloat16),
            pltpu.VMEM((k, k), f32),
            pltpu.VMEM((rows, k), jnp.bfloat16),
            pltpu.SemaphoreType.DMA((rows // TILE,)),
            pltpu.SemaphoreType.DMA,
        ],
        compiler_params=pltpu.CompilerParams(vmem_limit_bytes=36 * 2**20),
        name="finish",
    )(diag, cross, sketch, own_a, own_b, other_a, other_b)


def solution(mesh):
    in_specs = (P("leaf", "space", None), P("leaf", None), P())
    out_specs = (P("leaf", "space", None), P("leaf", None, None))
    return jax.shard_map(
        on_device, mesh=mesh, in_specs=in_specs, out_specs=out_specs, check_vma=False
    )
```
